256 devices in a mesh: clus: 16 (over y_hi, x, core), rep: 16 (over y_lo, z).
Axes of the slice: x: 4, y: 4 (y_hi: 2, y_lo: 2; y = y_hi * 2 + y_lo), z: 8, core: 2. Of those that a mesh axis runs over, the one named last changes fastest.
Arguments:
- embeddings: bfloat16 [65536, 768], P(('clus', 'rep')), may hold values from -6 to 6
- assignment: int32 [65536, 1], P(('clus', 'rep')), may hold values from 0 to 47; in each aligned block of 256 rows (0 to 255, 256 to 511, ...) at most 16 rows name the same one
- ordering: int32 [65536], P(('clus', 'rep')), may hold values from 0 to 65535, each once
Outputs:
- nearest: float32 [65536], P(('clus', 'rep'))
The draws below stay inside these ranges and needn't reach their ends.
Inputs may be any that keep to these rules, and one draw needn't show every extreme that they name: `assignment`: among the rows of one device (aligned blocks of 256 rows) no cluster is named more than 16 times, a bound that some block reaches. `ordering`: each position occurs once.
All inputs are finite; a program needn't handle non-finite values.
Results may differ from the reference program's by a relative error of at most 0.0014.
Values may be sent and summed in bfloat16 or wider, within the bound.
A program may use at most 64 MiB of HBM per device.

```python
import math
import jax
import jax.numpy as jnp
import numpy as np
from jax import lax

D = 768
R_DEV = 256
MOST = 16
CLUSTERS = 48
ROWS = 65536
N_CLUS = 16
N_REP = 16


def level_of(key, extent, pieces, low, top_value):
    level = 1.0
    for position, parts in pieces:
        draws = jax.random.uniform(jax.random.fold_in(jax.random.fold_in(key, 6), position), (parts,), jnp.float32, low / len(pieces), top_value / len(pieces))
        level = level * jnp.repeat(jnp.exp(draws), extent[position] // parts).reshape((-1,) + (1,) * (len(extent) - 1 - position))
    return level


def shared_out(key, own, number, rows, amount, top, bound, lean):
    sequence = jax.random.permutation(key, amount)
    heavy_load, usual = load_shares(amount, rows * top, bound, lean, True), load_shares(amount, rows * top, bound, lean, False)
    places = jnp.arange(amount)

    def named(lengths, turn):
        used = int((lengths > 0).sum())
        fixed = max(1, used // 4)
        shifted = fixed + (places - fixed + turn * (used - fixed)) % max(1, amount - fixed)
        return jnp.zeros((amount,), jnp.int32).at[sequence[jnp.where(places < fixed, places, shifted)]].set(jnp.asarray(lengths, jnp.int32))

    lengths = jnp.where(number % 4 == 0, named(heavy_load, number // 4), named(usual, number - number // 4 - 1))
    mixed = jax.random.permutation(jax.random.fold_in(own, 3), amount)
    donor, sink = mixed[0:amount // 2 * 2:2], mixed[1:amount // 2 * 2:2]
    room = jnp.minimum(lengths[donor] - 1, bound - lengths[sink]) // 2
    room = jnp.where((donor == sequence[0]) | (sink == sequence[0]) | (lengths[sink] == 0), 0, jnp.maximum(room, 0))
    shifted = jax.random.randint(jax.random.fold_in(own, 4), (amount // 2,), 0, 1 << 20) % (room + 1)
    lengths = lengths.at[donor].add(-shifted).at[sink].add(shifted)
    items = jnp.searchsorted(jnp.cumsum(lengths), jnp.arange(rows * top), side="right").astype(jnp.int32)
    table = items.reshape(top, rows).T
    table = table[jax.random.permutation(jax.random.fold_in(own, 1), rows)]
    turn = jax.random.randint(jax.random.fold_in(own, 2), (rows, 1), 0, top)
    return jnp.take_along_axis(table, (jnp.arange(top)[None, :] + turn) % top, axis=1)


def load_shares(number_of, total, bound, skew, full):
    portions = [(1 << 20) // math.isqrt(grade ** skew) + 1 for grade in range(1, number_of + 1)]
    largest = bound if full else min(bound, max(-(-total // number_of), total * portions[0] // sum(portions)))
    least = 1 if total - largest >= number_of - 1 else 0
    holding, rest = [largest] + [least] * (number_of - 1), total - largest - least * (number_of - 1)
    while rest > 0:
        movable = [i for i in range(1, number_of) if holding[i] < largest] or [i for i in range(1, number_of) if holding[i] < bound]
        pool, budget = sum([portions[i] for i in movable]), rest
        for i in movable:
            more = min(bound - holding[i], max(1, budget * portions[i] // pool), rest)
            holding[i] = holding[i] + more
            rest = rest - more
    return np.array(holding)


def noise(key, extent, width, limit, split=(), kind=jnp.bfloat16):
    level = level_of(key, extent, split, -0.22, 0.18) if split else 1.0
    entries = jax.random.normal(key, extent, jnp.float32) * width * level
    return jnp.minimum(jnp.maximum(entries, -limit), limit).astype(kind)


def setup_inputs(seed: int = 0) -> dict:
    streams_of = jax.random.split(jax.random.key(seed), 4)
    embeddings = noise(streams_of[0], (ROWS, D), 1.0, 6.0, ((0, 256),))
    assignment_keys = jax.random.split(jax.random.fold_in(streams_of[1], 1), ROWS // R_DEV)
    assignment_turns = jax.random.permutation(jax.random.fold_in(streams_of[1], 3), ROWS // R_DEV)
    assignment = jax.vmap(lambda own, number: shared_out(jax.random.fold_in(streams_of[1], 2), own, number, R_DEV, CLUSTERS, 1, MOST, 2))(assignment_keys, assignment_turns).reshape((ROWS, 1))
    ordering = jax.random.permutation(streams_of[2], ROWS).astype(jnp.int32)
    return dict(embeddings=embeddings, assignment=assignment, ordering=ordering)


vacant_key = 1073741824

def unit_rows(embeddings):
    widened = embeddings.astype(jnp.float32)
    scale = lax.rsqrt(lax.optimization_barrier(jnp.sum(widened * widened, axis=1, keepdims=True)) + 1e-06)
    return (widened * scale).astype(jnp.bfloat16)

def reference(embeddings, assignment, ordering):
    normed = unit_rows(embeddings).astype(jnp.float32)
    labels = assignment[:, 0].astype(jnp.int32)
    sort_key = labels * ROWS + ordering
    permuted = jnp.argsort(sort_key).astype(jnp.int32)
    lookback = N_CLUS * N_REP * MOST
    sorted_units = jnp.take(normed, permuted, axis=0)
    sorted_labels = jnp.take(labels, permuted)
    sorted_keys = jnp.take(ordering, permuted)
    padded_units = jnp.concatenate([jnp.zeros((lookback, D), jnp.float32), sorted_units], axis=0)
    padded_labels = jnp.concatenate([jnp.full((lookback,), -1, jnp.int32), sorted_labels])
    padded_keys = jnp.concatenate([jnp.full((lookback,), vacant_key, jnp.int32), sorted_keys.astype(jnp.int32)])
    block_rows = math.gcd(ROWS, 512)

    def one_block(first_row):
        queries = lax.dynamic_slice_in_dim(sorted_units, first_row, block_rows, 0)
        query_labels = lax.dynamic_slice_in_dim(sorted_labels, first_row, block_rows, 0)
        query_keys = lax.dynamic_slice_in_dim(sorted_keys, first_row, block_rows, 0)
        candidates = lax.dynamic_slice_in_dim(padded_units, first_row, lookback + block_rows, 0)
        cand_labels = lax.dynamic_slice_in_dim(padded_labels, first_row, lookback + block_rows, 0)
        cand_keys = lax.dynamic_slice_in_dim(padded_keys, first_row, lookback + block_rows, 0)
        scores = jnp.dot(queries, candidates.T, precision=lax.Precision.HIGHEST)
        earlier = (cand_labels[None, :] == query_labels[:, None]) & (cand_keys[None, :] < query_keys[:, None])
        return lax.optimization_barrier(jnp.max(jnp.where(earlier, scores, -1.0), axis=1))
    starts = jnp.arange(ROWS // block_rows, dtype=jnp.int32) * block_rows
    sorted_best = lax.map(one_block, starts).reshape(ROWS)
    return jnp.zeros((ROWS,), jnp.float32).at[permuted].set(sorted_best)
```

```python
import jax
import jax.numpy as jnp
from jax import lax
from jax.experimental import pallas as pl
from jax.experimental.pallas import tpu as pltpu
from jax.sharding import PartitionSpec as P

PLANE = ((0, 0), (1, 0), (0, 1), (3, 3), (2, 0), (0, 2), (3, 2), (2, 3), (2, 2), (1, 3))
LINES = (0, 1, 7, 2, 6, 3, 5, 4)
SOURCE = (None, 0, 0, 0, 1, 2, 3, 3, 6, 1)
LANDS = (None, 0, 0, 0, 2, 2, 2, 2, 4, 4)
ONE_WAY = (1, 2, 3, 6, 7, 9)
UNITS = (
    [(0, 0)],
    [(1, 0)],
    [(r, g) for r in (0, 1, 2) for g in (1, 2, 3)],
    [(3, g) for g in range(4)] + [(4, g) for g in (1, 2, 3)],
    [(r, g) for r in (0, 1, 3) for g in (4, 5, 6, 7)] + [(r, g) for r in (2, 4) for g in (6, 7)],
    [(5, g) for g in range(8)] + [(6, g) for g in (1, 2, 3, 6, 7)],
    [(r, g) for r in (0, 1, 3, 5) for g in (8, 9)] + [(r, 9) for r in (2, 4, 6)] + [(7, g) for g in range(10)],
)
STEPS = len(UNITS)
MESH = pl.DeviceIdType.MESH
LOWEST = -(2**31)
SPAN = 65536


def whereabouts():
    clus, rep = lax.axis_index("clus"), lax.axis_index("rep")
    return (clus // 2) % 4, (clus // 8) * 2 + rep // 8, rep % 8, clus % 2


def relative(dx, dy, dz, other):
    x, y, z, core = whereabouts()
    x, y, z, core = (x + dx) % 4, (y + dy) % 4, (z + dz) % 8, (core + other) % 2
    return ((y // 2) * 4 + x) * 2 + core, (y % 2) * 8 + z


def pick(table, n):
    value = jnp.int32(table[0])
    for i in range(1, len(table)):
        value = jnp.where(n == i, jnp.int32(table[i]), value)
    return value


def scores(lines, r, columns, c):
    return lax.dot_general(
        lines[r], columns[c], (((1,), (1,)), ((), ())), preferred_element_type=jnp.float32
    )


def keep_best(s, r, c, column_labels, line_place, line_order, line_best, column_best):
    label = column_labels[c]
    wide = []
    for left in (0, 128):
        p = label[:, left : left + 128]
        wide.append(
            [
                jnp.broadcast_to(p + (LOWEST + 1), (8, 128)),
                jnp.broadcast_to(p + LOWEST - 1, (8, 128)),
                jnp.broadcast_to((p & (SPAN - 1)) + LOWEST, (8, 128)),
                jnp.full((8, 128), -1.0, jnp.float32),
            ]
        )
    for top in range(0, 256, 8):
        mine, order = line_place[r, top : top + 8, :], line_order[r, top : top + 8, :]
        best = line_best[r, top : top + 8, :]
        for i, left in enumerate((0, 128)):
            after, before, other_order, down = wide[i]
            v = s[top : top + 8, left : left + 128]
            best = jnp.maximum(best, jnp.where(mine - after < order, v, -1.0))
            wide[i][3] = jnp.maximum(down, jnp.where(before - mine < other_order, v, -1.0))
        line_best[r, top : top + 8, :] = best
    for i, left in enumerate((0, 128)):
        here = column_best.at[c, :, pl.ds(left, 128)]
        here[...] = jnp.maximum(here[...], wide[i][3])


def kernel(
    rows_ref, cluster_ref, order_ref, out_ref,
    lines, columns, line_labels, column_labels, line_place, line_order, line_best, column_best, even, odd,
    line_answers, same_answers, other_answers, sibling_in, line_got, column_got,
    up_sent, up_got, down_sent, down_got, line_label_sent, line_label_got,
    plane_sent, plane_got, plane_label_sent, plane_label_got,
    across_sent, across_got, across_label_sent, across_label_got,
    line_answer_sent, line_answer_got, plane_answer_sent, plane_answer_got, sibling_sent, sibling_got,
):
    def remote(src, dst, sent, got, device):
        return pltpu.make_async_remote_copy(src, dst, sent, got, device_id=device, device_id_type=MESH)

    barrier = pltpu.get_barrier_semaphore()
    hello = {(0, 0, 1, 0), (0, 0, 7, 0), (0, 0, 0, 1)}
    for k in range(1, len(PLANE)):
        (x, y), (a, b) = PLANE[k], PLANE[SOURCE[k]]
        hello.add(((x - a) % 4, (y - b) % 4, 0, 0))
    for offset in sorted(hello):
        pl.semaphore_signal(barrier, inc=1, device_id=relative(*offset), device_id_type=MESH)

    for top in range(0, 256, 32):
        wide = rows_ref[top : top + 32, :].astype(jnp.float32)
        scale = lax.rsqrt(jnp.sum(wide * wide, axis=1, keepdims=True) + 1e-06)
        unit = (wide * scale).astype(jnp.bfloat16)
        lines[0, top : top + 32, :] = unit
        columns[0, top : top + 32, :] = unit
    place = cluster_ref[...] * SPAN + order_ref[...]
    line_labels[0] = place
    column_labels[0] = place
    pl.semaphore_wait(barrier, len(hello))

    def half(ref, slot, h):
        return ref.at[slot, pl.ds(pl.multiple_of(h * 128, 128), 128)]

    def up(n):
        k, h = n // 2, n % 2
        source = jnp.maximum(2 * k - 1, 0)
        return remote(half(lines, source, h), half(lines, 2 * k + 1, h), up_sent.at[n], up_got.at[n], relative(0, 0, 7, 0))

    def down(n):
        k, h = n // 2, 1 - n % 2
        return remote(
            half(lines, 2 * k, h), half(lines, jnp.minimum(2 * k + 2, 7), h),
            down_sent.at[n], down_got.at[n], relative(0, 0, 1, 0),
        )

    def up_label(k):
        source = jnp.maximum(2 * k - 1, 0)
        i = 2 * k + 1
        return remote(line_labels.at[source], line_labels.at[i], line_label_sent.at[i], line_label_got.at[i], relative(0, 0, 7, 0))

    def down_label(k):
        i = 2 * k + 2
        return remote(line_labels.at[2 * k], line_labels.at[i], line_label_sent.at[i], line_label_got.at[i], relative(0, 0, 1, 0))

    def between(k):
        (x, y), (a, b) = PLANE[k], PLANE[SOURCE[k]]
        return relative((a - x) % 4, (b - y) % 4, 0, 0)

    def plane(k, h):
        return remote(
            half(columns, 2 * SOURCE[k], h), half(columns, 2 * k, h),
            plane_sent.at[k, h], plane_got.at[k, h], between(k),
        )

    def plane_label(k):
        return remote(
            column_labels.at[2 * SOURCE[k]], column_labels.at[2 * k],
            plane_label_sent.at[k], plane_label_got.at[k], between(k),
        )

    def across(k):
        return remote(
            columns.at[2 * k], columns.at[2 * k + 1], across_sent.at[k], across_got.at[k], relative(0, 0, 0, 1)
        )

    def across_label(k):
        return remote(
            column_labels.at[2 * k], column_labels.at[2 * k + 1],
            across_label_sent.at[k], across_label_got.at[k], relative(0, 0, 0, 1),
        )

    first = [k for k in range(1, len(PLANE)) if LANDS[k] == 0]
    for h in (0, 1):
        up(jnp.int32(h)).start()
        down(jnp.int32(h)).start()
        for k in first:
            plane(k, h).start()
        if h == 0:
            up_label(jnp.int32(0)).start()
            down_label(jnp.int32(0)).start()
            for k in first:
                plane_label(k).start()
    across(0).start()
    across_label(0).start()

    line_best[...] = jnp.full(line_best.shape, -1.0, jnp.float32)
    column_best[...] = jnp.full(column_best.shape, -1.0, jnp.float32)
    odd[...] = jnp.full(odd.shape, -1.0, jnp.float32)

    def spread(r):
        for top in (0, 128):
            column = jnp.broadcast_to(line_labels[r, :, top : top + 128], (128, 128)).T
            line_place[r, top : top + 128, :] = column
            line_order[r, top : top + 128, :] = (column & (SPAN - 1)) + LOWEST

    spread(0)

    flat = [u for step in UNITS for u in step]
    starts = [sum(len(s) for s in UNITS[:n]) for n in range(STEPS + 1)]
    words = []
    for i in range(0, len(flat), 4):
        words.append(sum((r * 16 + g) << (7 * j) for j, (r, g) in enumerate(flat[i : i + 4])))

    def step(n, before):
        k, h = n // 2, n % 2
        up(n).wait_recv()
        down(n).wait_recv()

        @pl.when(n < STEPS - 2)
        def _():
            up(n + 2).start()
            down(n + 2).start()

        @pl.when(h == 0)
        def _():
            up_label(k).wait_recv()

            @pl.when(k < 3)
            def _():
                up_label(k + 1).start()
                down_label(k).wait_recv()

            @pl.when(k < 2)
            def _():
                down_label(k + 1).start()

        for at in (0, 2, 4):
            landing = [j for j in range(1, len(PLANE)) if LANDS[j] == at]

            @pl.when((n == at) | (n == at + 1))
            def _():
                for j in landing:
                    plane(j, h).wait_recv()
                for j in range(1, len(PLANE)):
                    if LANDS[j] == at + 2:
                        plane(j, h).start()

            @pl.when(n == at)
            def _():
                for j in landing:
                    plane_label(j).wait_recv()
                for j in range(1, len(PLANE)):
                    if LANDS[j] == at + 2:
                        plane_label(j).start()
                for j in [0] if at == 0 else [j for j in range(1, len(PLANE)) if LANDS[j] == at - 2]:
                    across(j).wait_recv()
                    across_label(j).wait_recv()

            @pl.when(n == at + 1)
            def _():
                for j in landing:
                    across(j).start()
                    across_label(j).start()

        @pl.when(n == 6)
        def _():
            for j in range(1, len(PLANE)):
                if LANDS[j] == 4:
                    across(j).wait_recv()
                    across_label(j).wait_recv()

            spread(7)

        @pl.when(h == 1)
        def _():
            spread(2 * k + 1)
            spread(2 * k + 2)

        def unit(u, carry):
            last_r, last_c = carry
            code = (pick(words, u // 4) >> ((u % 4) * 7)) & 127
            r, g = code >> 4, code & 15
            even[...] = scores(lines, r, columns, 2 * g)
            keep_best(odd, last_r, last_c, column_labels, line_place, line_order, line_best, column_best)
            odd[...] = scores(lines, r, columns, 2 * g + 1)
            keep_best(even, r, 2 * g, column_labels, line_place, line_order, line_best, column_best)
            return r, 2 * g + 1

        return lax.fori_loop(pick(starts, n), pick(starts[1:], n), unit, before)

    last_r, last_c = lax.fori_loop(0, STEPS, step, (jnp.int32(0), jnp.int32(0)))
    keep_best(odd, last_r, last_c, column_labels, line_place, line_order, line_best, column_best)

    def column_best_of(c):
        return jnp.max(column_best[c], axis=0, keepdims=True)

    for g in range(len(PLANE)):
        other_answers[g] = column_best_of(2 * g + 1)
    to_sibling = remote(other_answers, sibling_in, sibling_sent, sibling_got, relative(0, 0, 0, 1))
    to_sibling.start()

    def line_answer(r):
        return remote(
            line_answers.at[r], line_got.at[r], line_answer_sent.at[r], line_answer_got.at[r],
            relative(0, 0, LINES[r], 0),
        )

    def plane_answer(g):
        return remote(
            same_answers.at[g], column_got.at[g], plane_answer_sent.at[g], plane_answer_got.at[g],
            relative(*PLANE[g], 0, 0),
        )

    for r in range(8):
        line_answers[r] = jnp.max(line_best[r].T, axis=0, keepdims=True)
        if r:
            line_answer(r).start()
    to_sibling.wait_recv()
    for g in range(len(PLANE)):
        same_answers[g] = jnp.maximum(column_best_of(2 * g), sibling_in[g])
        if g:
            plane_answer(g).start()
    best = jnp.maximum(line_answers[0], same_answers[0])
    for r in range(1, 8):
        line_answer(r).wait_recv()
        best = jnp.maximum(best, line_got[r])
    for g in range(1, len(PLANE)):
        plane_answer(g).wait_recv()
        best = jnp.maximum(best, column_got[g])
    out_ref[...] = best

    to_sibling.wait_send()
    for r in range(1, 8):
        line_answer(r).wait_send()
    for g in range(1, len(PLANE)):
        plane_answer(g).wait_send()
        plane_label(g).wait_send()
        for h in (0, 1):
            plane(g, h).wait_send()
    for g in range(len(PLANE)):
        across(g).wait_send()
        across_label(g).wait_send()
    for n in range(STEPS):
        up(jnp.int32(n)).wait_send()
        down(jnp.int32(n)).wait_send()
    for k in range(4):
        up_label(jnp.int32(k)).wait_send()
    for k in range(3):
        down_label(jnp.int32(k)).wait_send()


def on_device(embeddings, assignment, ordering):
    rows, features = embeddings.shape
    plane = len(PLANE)
    dma = pltpu.SemaphoreType.DMA
    best = pl.pallas_call(
        kernel,
        out_shape=jax.ShapeDtypeStruct((1, rows), jnp.float32),
        in_specs=[pl.BlockSpec(memory_space=pltpu.VMEM)] * 3,
        out_specs=pl.BlockSpec(memory_space=pltpu.VMEM),
        scratch_shapes=[
            pltpu.VMEM((8, rows, features), jnp.bfloat16),
            pltpu.VMEM((2 * plane, rows, features), jnp.bfloat16),
            pltpu.VMEM((8, 1, rows), jnp.int32),
            pltpu.VMEM((2 * plane, 1, rows), jnp.int32),
            pltpu.VMEM((8, rows, 128), jnp.int32),
            pltpu.VMEM((8, rows, 128), jnp.int32),
            pltpu.VMEM((8, rows, 128), jnp.float32),
            pltpu.VMEM((2 * plane, 8, rows), jnp.float32),
            pltpu.VMEM((rows, rows), jnp.float32),
            pltpu.VMEM((rows, rows), jnp.float32),
            pltpu.VMEM((8, 1, rows), jnp.float32),
            pltpu.VMEM((plane, 1, rows), jnp.float32),
            pltpu.VMEM((plane, 1, rows), jnp.float32),
            pltpu.VMEM((plane, 1, rows), jnp.float32),
            pltpu.VMEM((8, 1, rows), jnp.float32),
            pltpu.VMEM((plane, 1, rows), jnp.float32),
            *[dma((STEPS,))] * 4,
            *[dma((8,))] * 2,
            *[dma((plane, 2))] * 2,
            *[dma((plane,))] * 2,
            *[dma((plane,))] * 4,
            *[dma((8,))] * 2,
            *[dma((plane,))] * 2,
            *[dma(())] * 2,
        ],
        compiler_params=pltpu.CompilerParams(
            collective_id=0, has_side_effects=True, vmem_limit_bytes=48 * 2**20
        ),
        cost_estimate=pl.CostEstimate(
            flops=2 * 136 * rows * rows * features, bytes_accessed=rows * features * 2, transcendentals=rows
        ),
    )(embeddings, assignment.reshape(1, rows), ordering.reshape(1, rows))
    return best.reshape(rows)


def solution(mesh):
    in_specs = (P(("clus", "rep"), None), P(("clus", "rep"), None), P(("clus", "rep")))
    out_specs = P(("clus", "rep"))
    return jax.shard_map(
        on_device, mesh=mesh, in_specs=in_specs, out_specs=out_specs, check_vma=False
    )
```

```python
import jax
import jax.numpy as jnp
from jax import lax
from jax.experimental import pallas as pl
from jax.experimental.pallas import tpu as pltpu
from jax.sharding import PartitionSpec as P

PLANE = ((0, 0), (1, 0), (0, 1), (3, 3), (2, 0), (0, 2), (3, 2), (2, 3), (2, 2), (1, 3))
LINES = (0, 1, 7, 2, 6, 3, 5, 4)
SOURCE = (None, 0, 0, 0, 1, 2, 3, 3, 6, 1)
LANDS = (None, 0, 0, 0, 2, 2, 2, 2, 4, 4)
GROUP = 4
UNITS = (
    [],
    [],
    [(r, g) for r in (0, 1) for g in range(4)],
    [(2, g) for g in (1, 2, 3)] + [(3, g) for g in range(4)] + [(4, 1)],
    [(4, 2), (4, 3)] + [(r, g) for r in (0, 1, 3) for g in (4, 5, 6, 7)] + [(2, 6), (2, 7)],
    [(4, 6), (4, 7)] + [(5, g) for g in range(8)] + [(6, 1), (6, 2)],
    [(6, 3), (6, 6), (6, 7)] + [(r, g) for r in (0, 1, 3, 5) for g in (8, 9)] + [(r, 9) for r in (2, 4, 6)]
    + [(7, g) for g in range(10)],
)
STEPS = len(UNITS)
MESH = pl.DeviceIdType.MESH
LOWEST = -(2**31)
SPAN = 65536


def whereabouts():
    clus, rep = lax.axis_index("clus"), lax.axis_index("rep")
    return (clus // 2) % 4, (clus // 8) * 2 + rep // 8, rep % 8, clus % 2


def relative(dx, dy, dz, other):
    x, y, z, core = whereabouts()
    x, y, z, core = (x + dx) % 4, (y + dy) % 4, (z + dz) % 8, (core + other) % 2
    return ((y // 2) * 4 + x) * 2 + core, (y % 2) * 8 + z


def pick(table, n):
    value = jnp.int32(table[0])
    for i in range(1, len(table)):
        value = jnp.where(n == i, jnp.int32(table[i]), value)
    return value


def scores(lines, r, columns, c):
    return lax.dot_general(
        lines[r], columns[c], (((1,), (1,)), ((), ())), preferred_element_type=jnp.float32
    )


def keep_best(s, r, c, column_labels, line_place, line_order, line_best, column_best):
    label = column_labels[c]
    wide = []
    for left in (0, 128):
        p = label[:, left : left + 128]
        wide.append(
            [
                jnp.broadcast_to(p + (LOWEST + 1), (8, 128)),
                jnp.broadcast_to(p + LOWEST - 1, (8, 128)),
                jnp.broadcast_to((p & (SPAN - 1)) + LOWEST, (8, 128)),
                jnp.full((8, 128), -1.0, jnp.float32),
            ]
        )
    for top in range(0, 256, 8):
        mine, order = line_place[r, top : top + 8, :], line_order[r, top : top + 8, :]
        best = line_best[r, top : top + 8, :]
        for i, left in enumerate((0, 128)):
            after, before, other_order, down = wide[i]
            v = s[top : top + 8, left : left + 128]
            best = jnp.maximum(best, jnp.where(mine - after < order, v, -1.0))
            wide[i][3] = jnp.maximum(down, jnp.where(before - mine < other_order, v, -1.0))
        line_best[r, top : top + 8, :] = best
    for i, left in enumerate((0, 128)):
        here = column_best.at[c, :, pl.ds(left, 128)]
        here[...] = jnp.maximum(here[...], wide[i][3])


def kernel(
    rows_ref, cluster_ref, order_ref, out_ref,
    lines, columns, line_labels, column_labels, line_place, line_order, line_best, column_best, even, odd,
    line_answers, same_answers, other_answers, sibling_in, line_got, column_got,
    up_sent, up_got, down_sent, down_got, line_label_sent, line_label_got,
    plane_sent, plane_got, plane_label_sent, plane_label_got,
    across_sent, across_got, across_label_sent, across_label_got,
    line_answer_sent, line_answer_got, plane_answer_sent, plane_answer_got, sibling_sent, sibling_got,
):
    def remote(src, dst, sent, got, device):
        return pltpu.make_async_remote_copy(src, dst, sent, got, device_id=device, device_id_type=MESH)

    barrier = pltpu.get_barrier_semaphore()
    hello = {(0, 0, 1, 0), (0, 0, 7, 0), (0, 0, 0, 1)}
    for k in range(1, len(PLANE)):
        (x, y), (a, b) = PLANE[k], PLANE[SOURCE[k]]
        hello.add(((x - a) % 4, (y - b) % 4, 0, 0))
    for offset in sorted(hello):
        pl.semaphore_signal(barrier, inc=1, device_id=relative(*offset), device_id_type=MESH)

    for top in range(0, 256, 32):
        wide = rows_ref[top : top + 32, :].astype(jnp.float32)
        scale = lax.rsqrt(jnp.sum(wide * wide, axis=1, keepdims=True) + 1e-06)
        unit = (wide * scale).astype(jnp.bfloat16)
        lines[0, top : top + 32, :] = unit
        columns[0, top : top + 32, :] = unit
    place = cluster_ref[...] * SPAN + order_ref[...]
    line_labels[0] = place
    column_labels[0] = place
    pl.semaphore_wait(barrier, len(hello))

    def half(ref, slot, h):
        return ref.at[slot, pl.ds(pl.multiple_of(h * 128, 128), 128)]

    def up(n):
        k, h = n // 2, n % 2
        source = jnp.maximum(2 * k - 1, 0)
        return remote(half(lines, source, h), half(lines, 2 * k + 1, h), up_sent.at[n], up_got.at[n], relative(0, 0, 7, 0))

    def down(n):
        k, h = n // 2, 1 - n % 2
        return remote(
            half(lines, 2 * k, h), half(lines, jnp.minimum(2 * k + 2, 7), h),
            down_sent.at[n], down_got.at[n], relative(0, 0, 1, 0),
        )

    def up_label(k):
        source = jnp.maximum(2 * k - 1, 0)
        i = 2 * k + 1
        return remote(line_labels.at[source], line_labels.at[i], line_label_sent.at[i], line_label_got.at[i], relative(0, 0, 7, 0))

    def down_label(k):
        i = 2 * k + 2
        return remote(line_labels.at[2 * k], line_labels.at[i], line_label_sent.at[i], line_label_got.at[i], relative(0, 0, 1, 0))

    def between(k):
        (x, y), (a, b) = PLANE[k], PLANE[SOURCE[k]]
        return relative((a - x) % 4, (b - y) % 4, 0, 0)

    def plane(k, h):
        return remote(
            half(columns, 2 * SOURCE[k], h), half(columns, 2 * k, h),
            plane_sent.at[k, h], plane_got.at[k, h], between(k),
        )

    def plane_label(k):
        return remote(
            column_labels.at[2 * SOURCE[k]], column_labels.at[2 * k],
            plane_label_sent.at[k], plane_label_got.at[k], between(k),
        )

    def across(k):
        return remote(
            columns.at[2 * k], columns.at[2 * k + 1], across_sent.at[k], across_got.at[k], relative(0, 0, 0, 1)
        )

    def across_label(k):
        return remote(
            column_labels.at[2 * k], column_labels.at[2 * k + 1],
            across_label_sent.at[k], across_label_got.at[k], relative(0, 0, 0, 1),
        )

    first = [k for k in range(1, len(PLANE)) if LANDS[k] == 0]
    for h in (0, 1):
        up(jnp.int32(h)).start()
        down(jnp.int32(h)).start()
        for k in first:
            plane(k, h).start()
        if h == 0:
            up_label(jnp.int32(0)).start()
            down_label(jnp.int32(0)).start()
            for k in first:
                plane_label(k).start()
    across(0).start()
    across_label(0).start()

    line_best[...] = jnp.full(line_best.shape, -1.0, jnp.float32)
    column_best[...] = jnp.full(column_best.shape, -1.0, jnp.float32)
    odd[...] = jnp.full(odd.shape, -1.0, jnp.float32)

    def spread(r):
        for top in (0, 128):
            column = jnp.broadcast_to(line_labels[r, :, top : top + 128], (128, 128)).T
            line_place[r, top : top + 128, :] = column
            line_order[r, top : top + 128, :] = (column & (SPAN - 1)) + LOWEST

    spread(0)

    flat = [u for step in UNITS for u in step]
    starts = [sum(len(s) for s in UNITS[:n]) // GROUP for n in range(STEPS + 1)]
    words = []
    for i in range(0, len(flat), GROUP):
        words.append(sum((r * 16 + g) << (7 * j) for j, (r, g) in enumerate(flat[i : i + GROUP])))

    def step(n, before):
        k, h = n // 2, n % 2
        up(n).wait_recv()
        down(n).wait_recv()

        @pl.when(n < STEPS - 2)
        def _():
            up(n + 2).start()
            down(n + 2).start()

        @pl.when(h == 0)
        def _():
            up_label(k).wait_recv()

            @pl.when(k < 3)
            def _():
                up_label(k + 1).start()
                down_label(k).wait_recv()

            @pl.when(k < 2)
            def _():
                down_label(k + 1).start()

        for at in (0, 2, 4):
            landing = [j for j in range(1, len(PLANE)) if LANDS[j] == at]

            @pl.when((n == at) | (n == at + 1))
            def _():
                for j in landing:
                    plane(j, h).wait_recv()
                for j in range(1, len(PLANE)):
                    if LANDS[j] == at + 2:
                        plane(j, h).start()

            @pl.when(n == at)
            def _():
                for j in landing:
                    plane_label(j).wait_recv()
                for j in range(1, len(PLANE)):
                    if LANDS[j] == at + 2:
                        plane_label(j).start()
                for j in [0] if at == 0 else [j for j in range(1, len(PLANE)) if LANDS[j] == at - 2]:
                    across(j).wait_recv()
                    across_label(j).wait_recv()

            @pl.when(n == at + 1)
            def _():
                for j in landing:
                    across(j).start()
                    across_label(j).start()

        @pl.when(n == 6)
        def _():
            for j in range(1, len(PLANE)):
                if LANDS[j] == 4:
                    across(j).wait_recv()
                    across_label(j).wait_recv()

            spread(7)

        @pl.when(h == 1)
        def _():
            spread(2 * k + 1)
            spread(2 * k + 2)

        def group(u, carry):
            last_r, last_c = carry
            word = pick(words, u)
            for i in range(GROUP):
                code = (word >> (7 * i)) & 127
                r, g = code >> 4, code & 15
                even[...] = scores(lines, r, columns, 2 * g)
                keep_best(odd, last_r, last_c, column_labels, line_place, line_order, line_best, column_best)
                odd[...] = scores(lines, r, columns, 2 * g + 1)
                keep_best(even, r, 2 * g, column_labels, line_place, line_order, line_best, column_best)
                last_r, last_c = r, 2 * g + 1
            return last_r, last_c

        return lax.fori_loop(pick(starts, n), pick(starts[1:], n), group, before)

    last_r, last_c = lax.fori_loop(0, STEPS, step, (jnp.int32(0), jnp.int32(0)))
    keep_best(odd, last_r, last_c, column_labels, line_place, line_order, line_best, column_best)

    def column_best_of(c):
        return jnp.max(column_best[c], axis=0, keepdims=True)

    for g in range(len(PLANE)):
        other_answers[g] = column_best_of(2 * g + 1)
    to_sibling = remote(other_answers, sibling_in, sibling_sent, sibling_got, relative(0, 0, 0, 1))
    to_sibling.start()

    def line_answer(r):
        return remote(
            line_answers.at[r], line_got.at[r], line_answer_sent.at[r], line_answer_got.at[r],
            relative(0, 0, LINES[r], 0),
        )

    def plane_answer(g):
        return remote(
            same_answers.at[g], column_got.at[g], plane_answer_sent.at[g], plane_answer_got.at[g],
            relative(*PLANE[g], 0, 0),
        )

    for r in range(8):
        line_answers[r] = jnp.max(line_best[r].T, axis=0, keepdims=True)
        if r:
            line_answer(r).start()
    to_sibling.wait_recv()
    for g in range(len(PLANE)):
        same_answers[g] = jnp.maximum(column_best_of(2 * g), sibling_in[g])
        if g:
            plane_answer(g).start()
    best = jnp.maximum(line_answers[0], same_answers[0])
    for r in range(1, 8):
        line_answer(r).wait_recv()
        best = jnp.maximum(best, line_got[r])
    for g in range(1, len(PLANE)):
        plane_answer(g).wait_recv()
        best = jnp.maximum(best, column_got[g])
    out_ref[...] = best

    to_sibling.wait_send()
    for r in range(1, 8):
        line_answer(r).wait_send()
    for g in range(1, len(PLANE)):
        plane_answer(g).wait_send()
        plane_label(g).wait_send()
        for h in (0, 1):
            plane(g, h).wait_send()
    for g in range(len(PLANE)):
        across(g).wait_send()
        across_label(g).wait_send()
    for n in range(STEPS):
        up(jnp.int32(n)).wait_send()
        down(jnp.int32(n)).wait_send()
    for k in range(4):
        up_label(jnp.int32(k)).wait_send()
    for k in range(3):
        down_label(jnp.int32(k)).wait_send()


def on_device(embeddings, assignment, ordering):
    rows, features = embeddings.shape
    plane = len(PLANE)
    dma = pltpu.SemaphoreType.DMA
    best = pl.pallas_call(
        kernel,
        out_shape=jax.ShapeDtypeStruct((1, rows), jnp.float32),
        in_specs=[pl.BlockSpec(memory_space=pltpu.VMEM)] * 3,
        out_specs=pl.BlockSpec(memory_space=pltpu.VMEM),
        scratch_shapes=[
            pltpu.VMEM((8, rows, features), jnp.bfloat16),
            pltpu.VMEM((2 * plane, rows, features), jnp.bfloat16),
            pltpu.VMEM((8, 1, rows), jnp.int32),
            pltpu.VMEM((2 * plane, 1, rows), jnp.int32),
            pltpu.VMEM((8, rows, 128), jnp.int32),
            pltpu.VMEM((8, rows, 128), jnp.int32),
            pltpu.VMEM((8, rows, 128), jnp.float32),
            pltpu.VMEM((2 * plane, 8, rows), jnp.float32),
            pltpu.VMEM((rows, rows), jnp.float32),
            pltpu.VMEM((rows, rows), jnp.float32),
            pltpu.VMEM((8, 1, rows), jnp.float32),
            pltpu.VMEM((plane, 1, rows), jnp.float32),
            pltpu.VMEM((plane, 1, rows), jnp.float32),
            pltpu.VMEM((plane, 1, rows), jnp.float32),
            pltpu.VMEM((8, 1, rows), jnp.float32),
            pltpu.VMEM((plane, 1, rows), jnp.float32),
            *[dma((STEPS,))] * 4,
            *[dma((8,))] * 2,
            *[dma((plane, 2))] * 2,
            *[dma((plane,))] * 2,
            *[dma((plane,))] * 4,
            *[dma((8,))] * 2,
            *[dma((plane,))] * 2,
            *[dma(())] * 2,
        ],
        compiler_params=pltpu.CompilerParams(
            collective_id=0, has_side_effects=True, vmem_limit_bytes=48 * 2**20
        ),
        cost_estimate=pl.CostEstimate(
            flops=2 * 136 * rows * rows * features, bytes_accessed=rows * features * 2, transcendentals=rows
        ),
    )(embeddings, assignment.reshape(1, rows), ordering.reshape(1, rows))
    return best.reshape(rows)


def solution(mesh):
    in_specs = (P(("clus", "rep"), None), P(("clus", "rep"), None), P(("clus", "rep")))
    out_specs = P(("clus", "rep"))
    return jax.shard_map(
        on_device, mesh=mesh, in_specs=in_specs, out_specs=out_specs, check_vma=False
    )
```

```python
import jax
import jax.numpy as jnp
from jax import lax
from jax.experimental import pallas as pl
from jax.experimental.pallas import tpu as pltpu
from jax.sharding import PartitionSpec as P

PLANE = ((0, 0), (1, 0), (0, 1), (3, 3), (2, 0), (0, 2), (3, 2), (2, 3), (2, 2), (1, 3))
LINES = (0, 1, 7, 2, 6, 3, 5, 4)
SOURCE = (None, 0, 0, 0, 1, 2, 3, 3, 6, 1)
LANDS = (None, 0, 0, 0, 2, 2, 2, 2, 4, 4)
GROUP = 4
UNITS = (
    ([], []),
    ([], [(r, g) for r in (0, 1) for g in range(4)]),
    ([], []),
    (
        [(2, g) for g in (1, 2, 3)] + [(3, g) for g in range(4)] + [(4, 1)],
        [(4, 2), (4, 3), (2, 6), (2, 7)] + [(0, g) for g in (4, 5, 6, 7)],
    ),
    ([(r, g) for r in (1, 3) for g in (4, 5, 6, 7)], []),
    (
        [(4, 6), (4, 7)] + [(5, g) for g in range(8)] + [(6, 1), (6, 2)],
        [(6, 3), (6, 6), (6, 7)] + [(r, g) for r in (0, 1, 3, 5) for g in (8, 9)] + [(2, 9)],
    ),
    ([(4, 9), (6, 9), (7, 0), (7, 1)], [(7, g) for g in range(2, 10)]),
)
STEPS = len(UNITS)
MESH = pl.DeviceIdType.MESH
LOWEST = -(2**31)
SPAN = 65536


def whereabouts():
    clus, rep = lax.axis_index("clus"), lax.axis_index("rep")
    return (clus // 2) % 4, (clus // 8) * 2 + rep // 8, rep % 8, clus % 2


def relative(dx, dy, dz, other):
    x, y, z, core = whereabouts()
    x, y, z, core = (x + dx) % 4, (y + dy) % 4, (z + dz) % 8, (core + other) % 2
    return ((y // 2) * 4 + x) * 2 + core, (y % 2) * 8 + z


def pick(table, n):
    value = jnp.int32(table[0])
    for i in range(1, len(table)):
        value = jnp.where(n == i, jnp.int32(table[i]), value)
    return value


def scores(lines, r, columns, c):
    return lax.dot_general(
        lines[r], columns[c], (((1,), (1,)), ((), ())), preferred_element_type=jnp.float32
    )


def keep_best(s, r, c, column_labels, line_place, line_order, line_best, column_best):
    label = column_labels[c]
    wide = []
    for left in (0, 128):
        p = label[:, left : left + 128]
        wide.append(
            [
                jnp.broadcast_to(p + (LOWEST + 1), (8, 128)),
                jnp.broadcast_to(p + LOWEST - 1, (8, 128)),
                jnp.broadcast_to((p & (SPAN - 1)) + LOWEST, (8, 128)),
                jnp.full((8, 128), -1.0, jnp.float32),
            ]
        )
    for top in range(0, 256, 8):
        mine, order = line_place[r, top : top + 8, :], line_order[r, top : top + 8, :]
        best = line_best[r, top : top + 8, :]
        for i, left in enumerate((0, 128)):
            after, before, other_order, down = wide[i]
            v = s[top : top + 8, left : left + 128]
            best = jnp.maximum(best, jnp.where(mine - after < order, v, -1.0))
            wide[i][3] = jnp.maximum(down, jnp.where(before - mine < other_order, v, -1.0))
        line_best[r, top : top + 8, :] = best
    for i, left in enumerate((0, 128)):
        here = column_best.at[c, :, pl.ds(left, 128)]
        here[...] = jnp.maximum(here[...], wide[i][3])


def kernel(
    rows_hbm, cluster_hbm, order_hbm, out_ref, rows_ref, cluster_ref, order_ref, loaded,
    lines, columns, line_labels, column_labels, line_place, line_order, line_best, column_best, even, odd,
    line_answers, same_answers, other_answers, sibling_in, line_got, column_got,
    up_sent, up_got, down_sent, down_got, line_label_sent, line_label_got,
    plane_sent, plane_got, plane_label_sent, plane_label_got,
    across_sent, across_got, across_label_sent, across_label_got,
    line_answer_sent, line_answer_got, plane_answer_sent, plane_answer_got, sibling_sent, sibling_got,
):
    def remote(src, dst, sent, got, device):
        return pltpu.make_async_remote_copy(src, dst, sent, got, device_id=device, device_id_type=MESH)

    loads = [
        pltpu.make_async_copy(src, dst, loaded.at[i])
        for i, (src, dst) in enumerate(((rows_hbm, rows_ref), (cluster_hbm, cluster_ref), (order_hbm, order_ref)))
    ]
    for load in loads:
        load.start()
    barrier = pltpu.get_barrier_semaphore()
    hello = {(0, 0, 1, 0), (0, 0, 7, 0), (0, 0, 0, 1)}
    for k in range(1, len(PLANE)):
        (x, y), (a, b) = PLANE[k], PLANE[SOURCE[k]]
        hello.add(((x - a) % 4, (y - b) % 4, 0, 0))
    for offset in sorted(hello):
        pl.semaphore_signal(barrier, inc=1, device_id=relative(*offset), device_id_type=MESH)

    loads[0].wait()
    for top in range(0, 256, 32):
        wide = rows_ref[top : top + 32, :].astype(jnp.float32)
        scale = lax.rsqrt(jnp.sum(wide * wide, axis=1, keepdims=True) + 1e-06)
        unit = (wide * scale).astype(jnp.bfloat16)
        lines[0, top : top + 32, :] = unit
        columns[0, top : top + 32, :] = unit
    loads[1].wait()
    loads[2].wait()
    place = cluster_ref[...] * SPAN + order_ref[...]
    line_labels[0] = place
    column_labels[0] = place
    pl.semaphore_wait(barrier, len(hello))

    def half(ref, slot, h):
        return ref.at[slot, pl.ds(pl.multiple_of(h * 128, 128), 128)]

    def up(n):
        k, h = n // 2, n % 2
        source = jnp.maximum(2 * k - 1, 0)
        return remote(half(lines, source, h), half(lines, 2 * k + 1, h), up_sent.at[n], up_got.at[n], relative(0, 0, 7, 0))

    def down(n):
        k, h = n // 2, 1 - n % 2
        return remote(
            half(lines, 2 * k, h), half(lines, jnp.minimum(2 * k + 2, 7), h),
            down_sent.at[n], down_got.at[n], relative(0, 0, 1, 0),
        )

    def up_label(k):
        source = jnp.maximum(2 * k - 1, 0)
        i = 2 * k + 1
        return remote(line_labels.at[source], line_labels.at[i], line_label_sent.at[i], line_label_got.at[i], relative(0, 0, 7, 0))

    def down_label(k):
        i = 2 * k + 2
        return remote(line_labels.at[2 * k], line_labels.at[i], line_label_sent.at[i], line_label_got.at[i], relative(0, 0, 1, 0))

    def between(k):
        (x, y), (a, b) = PLANE[k], PLANE[SOURCE[k]]
        return relative((a - x) % 4, (b - y) % 4, 0, 0)

    def plane(k, h):
        return remote(
            half(columns, 2 * SOURCE[k], h), half(columns, 2 * k, h),
            plane_sent.at[k, h], plane_got.at[k, h], between(k),
        )

    def plane_label(k):
        return remote(
            column_labels.at[2 * SOURCE[k]], column_labels.at[2 * k],
            plane_label_sent.at[k], plane_label_got.at[k], between(k),
        )

    def across(k):
        return remote(
            columns.at[2 * k], columns.at[2 * k + 1], across_sent.at[k], across_got.at[k], relative(0, 0, 0, 1)
        )

    def across_label(k):
        return remote(
            column_labels.at[2 * k], column_labels.at[2 * k + 1],
            across_label_sent.at[k], across_label_got.at[k], relative(0, 0, 0, 1),
        )

    first = [k for k in range(1, len(PLANE)) if LANDS[k] == 0]
    for h in (0, 1):
        up(jnp.int32(h)).start()
        down(jnp.int32(h)).start()
        for k in first:
            plane(k, h).start()
        if h == 0:
            up_label(jnp.int32(0)).start()
            down_label(jnp.int32(0)).start()
            for k in first:
                plane_label(k).start()
    across(0).start()
    across_label(0).start()

    line_best[...] = jnp.full(line_best.shape, -1.0, jnp.float32)
    column_best[...] = jnp.full(column_best.shape, -1.0, jnp.float32)
    odd[...] = jnp.full(odd.shape, -1.0, jnp.float32)

    def spread(r):
        for top in (0, 128):
            column = jnp.broadcast_to(line_labels[r, :, top : top + 128], (128, 128)).T
            line_place[r, top : top + 128, :] = column
            line_order[r, top : top + 128, :] = (column & (SPAN - 1)) + LOWEST

    spread(0)

    lists = [part for both in UNITS for part in both]
    flat = [u for part in lists for u in part]
    starts = [sum(len(part) for part in lists[:m]) // GROUP for m in range(len(lists) + 1)]
    words = []
    for i in range(0, len(flat), GROUP):
        words.append(sum((r * 16 + g) << (7 * j) for j, (r, g) in enumerate(flat[i : i + GROUP])))

    def line_answer(r):
        return remote(
            line_answers.at[r], line_got.at[r], line_answer_sent.at[r], line_answer_got.at[r],
            relative(0, 0, LINES[r], 0),
        )

    def answer_line(r):
        line_answers[r] = jnp.max(line_best[r].T, axis=0, keepdims=True)
        if r:
            line_answer(r).start()

    def arrivals(n):
        k, h = n // 2, n % 2
        up(n).wait_recv()
        down(n).wait_recv()

        @pl.when(n < STEPS - 2)
        def _():
            up(n + 2).start()
            down(n + 2).start()

        for at in (0, 2, 4):
            landing = [j for j in range(1, len(PLANE)) if LANDS[j] == at]
            onward = [j for j in range(1, len(PLANE)) if LANDS[j] == at + 2]

            @pl.when((n == at) | (n == at + 1))
            def _():
                for j in landing:
                    plane(j, h).wait_recv()
                for j in onward:
                    plane(j, h).start()

            @pl.when(n == at)
            def _():
                for j in landing:
                    plane_label(j).wait_recv()
                for j in onward:
                    plane_label(j).start()

            @pl.when(n == at + 1)
            def _():
                for j in landing:
                    across(j).start()
                    across_label(j).start()

        @pl.when(h == 0)
        def _():
            up_label(k).wait_recv()

            @pl.when(k < 3)
            def _():
                up_label(k + 1).start()
                down_label(k).wait_recv()

            @pl.when(k < 2)
            def _():
                down_label(k + 1).start()

        @pl.when(n == 6)
        def _():
            spread(7)

        @pl.when(h == 1)
        def _():
            spread(2 * k + 1)
            spread(2 * k + 2)

    def from_sibling(n):
        for at in (0, 1, 3, 5):

            @pl.when(n == at)
            def _():
                for j in range(len(PLANE)):
                    if (LANDS[j] + 1 if j else 0) == at:
                        across(j).wait_recv()
                        across_label(j).wait_recv()

    def step(m, before):
        n = m // 2

        @pl.when(m % 2 == 0)
        def _():
            arrivals(n)

        @pl.when(m % 2 == 1)
        def _():
            from_sibling(n)

        def group(u, carry):
            last_r, last_c = carry
            word = pick(words, u)
            for i in range(GROUP):
                code = (word >> (7 * i)) & 127
                r, g = code >> 4, code & 15
                even[...] = scores(lines, r, columns, 2 * g)
                keep_best(odd, last_r, last_c, column_labels, line_place, line_order, line_best, column_best)
                odd[...] = scores(lines, r, columns, 2 * g + 1)
                keep_best(even, r, 2 * g, column_labels, line_place, line_order, line_best, column_best)
                last_r, last_c = r, 2 * g + 1
            return last_r, last_c

        return lax.fori_loop(pick(starts, m), pick(starts[1:], m), group, before)

    last_r, last_c = lax.fori_loop(0, len(lists), step, (jnp.int32(0), jnp.int32(0)))
    keep_best(odd, last_r, last_c, column_labels, line_place, line_order, line_best, column_best)

    def column_best_of(c):
        return jnp.max(column_best[c], axis=0, keepdims=True)

    for g in range(len(PLANE)):
        other_answers[g] = column_best_of(2 * g + 1)
    to_sibling = remote(other_answers, sibling_in, sibling_sent, sibling_got, relative(0, 0, 0, 1))
    to_sibling.start()

    def plane_answer(g):
        return remote(
            same_answers.at[g], column_got.at[g], plane_answer_sent.at[g], plane_answer_got.at[g],
            relative(*PLANE[g], 0, 0),
        )

    for r in range(8):
        answer_line(r)
    to_sibling.wait_recv()
    for g in range(len(PLANE)):
        same_answers[g] = jnp.maximum(column_best_of(2 * g), sibling_in[g])
        if g:
            plane_answer(g).start()
    best = jnp.maximum(line_answers[0], same_answers[0])
    for r in range(1, 8):
        line_answer(r).wait_recv()
        best = jnp.maximum(best, line_got[r])
    for g in range(1, len(PLANE)):
        plane_answer(g).wait_recv()
        best = jnp.maximum(best, column_got[g])
    out_ref[...] = best

    to_sibling.wait_send()
    for r in range(1, 8):
        line_answer(r).wait_send()
    for g in range(1, len(PLANE)):
        plane_answer(g).wait_send()
        plane_label(g).wait_send()
        for h in (0, 1):
            plane(g, h).wait_send()
    for g in range(len(PLANE)):
        across(g).wait_send()
        across_label(g).wait_send()
    for n in range(STEPS):
        up(jnp.int32(n)).wait_send()
        down(jnp.int32(n)).wait_send()
    for k in range(4):
        up_label(jnp.int32(k)).wait_send()
    for k in range(3):
        down_label(jnp.int32(k)).wait_send()


def on_device(embeddings, assignment, ordering):
    rows, features = embeddings.shape
    plane = len(PLANE)
    dma = pltpu.SemaphoreType.DMA
    best = pl.pallas_call(
        kernel,
        out_shape=jax.ShapeDtypeStruct((1, rows), jnp.float32),
        in_specs=[pl.BlockSpec(memory_space=pltpu.HBM)] * 3,
        out_specs=pl.BlockSpec(memory_space=pltpu.VMEM),
        scratch_shapes=[
            pltpu.VMEM((rows, features), jnp.bfloat16),
            pltpu.VMEM((1, rows), jnp.int32),
            pltpu.VMEM((1, rows), jnp.int32),
            dma((3,)),
            pltpu.VMEM((8, rows, features), jnp.bfloat16),
            pltpu.VMEM((2 * plane, rows, features), jnp.bfloat16),
            pltpu.VMEM((8, 1, rows), jnp.int32),
            pltpu.VMEM((2 * plane, 1, rows), jnp.int32),
            pltpu.VMEM((8, rows, 128), jnp.int32),
            pltpu.VMEM((8, rows, 128), jnp.int32),
            pltpu.VMEM((8, rows, 128), jnp.float32),
            pltpu.VMEM((2 * plane, 8, rows), jnp.float32),
            pltpu.VMEM((rows, rows), jnp.float32),
            pltpu.VMEM((rows, rows), jnp.float32),
            pltpu.VMEM((8, 1, rows), jnp.float32),
            pltpu.VMEM((plane, 1, rows), jnp.float32),
            pltpu.VMEM((plane, 1, rows), jnp.float32),
            pltpu.VMEM((plane, 1, rows), jnp.float32),
            pltpu.VMEM((8, 1, rows), jnp.float32),
            pltpu.VMEM((plane, 1, rows), jnp.float32),
            *[dma((STEPS,))] * 4,
            *[dma((8,))] * 2,
            *[dma((plane, 2))] * 2,
            *[dma((plane,))] * 2,
            *[dma((plane,))] * 4,
            *[dma((8,))] * 2,
            *[dma((plane,))] * 2,
            *[dma(())] * 2,
        ],
        compiler_params=pltpu.CompilerParams(
            collective_id=0, has_side_effects=True, vmem_limit_bytes=48 * 2**20
        ),
        cost_estimate=pl.CostEstimate(
            flops=2 * 136 * rows * rows * features, bytes_accessed=rows * features * 2, transcendentals=rows
        ),
    )(embeddings, assignment.reshape(1, rows), ordering.reshape(1, rows))
    return best.reshape(rows)


def solution(mesh):
    in_specs = (P(("clus", "rep"), None), P(("clus", "rep"), None), P(("clus", "rep")))
    out_specs = P(("clus", "rep"))
    return jax.shard_map(
        on_device, mesh=mesh, in_specs=in_specs, out_specs=out_specs, check_vma=False
    )
```

```python
import jax
import jax.numpy as jnp
from jax import lax
from jax.experimental import pallas as pl
from jax.experimental.pallas import tpu as pltpu
from jax.sharding import PartitionSpec as P

PLANE = ((0, 0), (1, 0), (0, 1), (3, 3), (2, 0), (0, 2), (3, 2), (2, 3), (2, 2), (1, 3))
LINES = (0, 1, 7, 2, 6, 3, 5, 4)
SOURCE = (None, 0, 0, 0, 1, 2, 3, 3, 6, 1)
LANDS = (None, 0, 0, 0, 2, 2, 2, 2, 4, 4)


def both(*units):
    return [(r, 2 * g + c, 0) for r, g in units for c in (0, 1)]


BY_Z, BY_X, BY_Y = 1, 2, 3
GROUP = 8
TILES = (
    [(0, 1, 0)] + both(*((0, g) for g in (1, 2, 3)), *((1, g) for g in range(4)), (2, 1), (2, 2), (2, 3))
    + both(*((3, g) for g in range(4)), *((4, g) for g in (1, 2, 3)))
    + [(0, 8, BY_X), (0, 10, BY_Y)] + both((2, 6), (2, 7), (0, 6), (0, 7), *((1, g) for g in (4, 5, 6, 7)))
    + both(*((3, g) for g in (4, 5, 6, 7)), (4, 6), (4, 7))
    + both(*((5, g) for g in range(8)), *((6, g) for g in (1, 2, 3, 6, 7)))
    + [(0, 16, BY_X)] + both((0, 9), *((r, g) for r in (1, 3, 5) for g in (8, 9)), (2, 9), (4, 9), (6, 9))
    + both(*((7, g) for g in (1, 2, 3, 6, 7, 9))) + [(7, 2 * g, BY_Z) for g in (0, 4, 5, 8)]
)
GROUPS = ((0, 0), (0, 2), (0, 0), (2, 2), (2, 0), (3, 3), (2, 0))
STEPS = len(GROUPS)
MESH = pl.DeviceIdType.MESH
LOWEST, HIGHEST = -(2**31), 2**31 - 1
SPAN = 65536


def whereabouts():
    clus, rep = lax.axis_index("clus"), lax.axis_index("rep")
    return (clus // 2) % 4, (clus // 8) * 2 + rep // 8, rep % 8, clus % 2


def relative(dx, dy, dz, other):
    x, y, z, core = whereabouts()
    x, y, z, core = (x + dx) % 4, (y + dy) % 4, (z + dz) % 8, (core + other) % 2
    return ((y // 2) * 4 + x) * 2 + core, (y % 2) * 8 + z


def pick(table, n):
    value = jnp.int32(table[0])
    for i in range(1, len(table)):
        value = jnp.where(n == i, jnp.int32(table[i]), value)
    return value


def scores(lines, r, columns, c):
    return lax.dot_general(
        lines[r], columns[c], (((1,), (1,)), ((), ())), preferred_element_type=jnp.float32
    )


def keep_best(s, r, c, column_labels, line_place, line_order, line_best, column_best, same_rows=False):
    label = column_labels[c]
    wide = []
    for left in (0, 128):
        p = label[:, left : left + 128]
        wide.append(
            [
                jnp.broadcast_to(p + LOWEST, (8, 128)),
                jnp.broadcast_to(HIGHEST - (p & (SPAN - 1)), (8, 128)),
                jnp.full((8, 128), -1.0, jnp.float32),
            ]
        )
    for top in range(0, 256, 8):
        mine, order = line_place[r, top : top + 8, :], line_order[r, top : top + 8, :]
        best = line_best[r, top : top + 8, :]
        for i, left in enumerate((0, 128)):
            theirs, limit, down = wide[i]
            ahead = mine - theirs
            v = s[top : top + 8, left : left + 128]
            earlier = ahead <= order
            if same_rows:
                earlier &= ahead != LOWEST
            best = jnp.maximum(best, jnp.where(earlier, v, -1.0))
            wide[i][2] = jnp.maximum(down, jnp.where(ahead > limit, v, -1.0))
        line_best[r, top : top + 8, :] = best
    for i, left in enumerate((0, 128)):
        here = column_best.at[c, :, pl.ds(left, 128)]
        here[...] = jnp.maximum(here[...], wide[i][2])


def kernel(
    rows_hbm, cluster_hbm, order_hbm, out_ref, rows_ref, cluster_ref, order_ref, loaded,
    lines, columns, line_labels, column_labels, line_place, line_order, line_best, column_best, even, odd,
    line_answers, same_answers, other_answers, sibling_in, line_got, column_got,
    up_sent, up_got, down_sent, down_got, line_label_sent, line_label_got,
    plane_sent, plane_got, plane_label_sent, plane_label_got,
    across_sent, across_got, across_label_sent, across_label_got,
    line_answer_sent, line_answer_got, plane_answer_sent, plane_answer_got, sibling_sent, sibling_got,
):
    def remote(src, dst, sent, got, device):
        return pltpu.make_async_remote_copy(src, dst, sent, got, device_id=device, device_id_type=MESH)

    loads = [
        pltpu.make_async_copy(src, dst, loaded.at[i])
        for i, (src, dst) in enumerate(((rows_hbm, rows_ref), (cluster_hbm, cluster_ref), (order_hbm, order_ref)))
    ]
    for load in loads:
        load.start()
    barrier = pltpu.get_barrier_semaphore()
    hello = {(0, 0, 1, 0), (0, 0, 7, 0), (0, 0, 0, 1)}
    for k in range(1, len(PLANE)):
        (x, y), (a, b) = PLANE[k], PLANE[SOURCE[k]]
        hello.add(((x - a) % 4, (y - b) % 4, 0, 0))
    for offset in sorted(hello):
        pl.semaphore_signal(barrier, inc=1, device_id=relative(*offset), device_id_type=MESH)

    loads[0].wait()
    for top in range(0, 256, 32):
        wide = rows_ref[top : top + 32, :].astype(jnp.float32)
        scale = lax.rsqrt(jnp.sum(wide * wide, axis=1, keepdims=True) + 1e-06)
        unit = (wide * scale).astype(jnp.bfloat16)
        lines[0, top : top + 32, :] = unit
        columns[0, top : top + 32, :] = unit
    loads[1].wait()
    loads[2].wait()
    place = cluster_ref[...] * SPAN + order_ref[...]
    line_labels[0] = place
    column_labels[0] = place
    pl.semaphore_wait(barrier, len(hello))

    def half(ref, slot, h):
        return ref.at[slot, pl.ds(pl.multiple_of(h * 128, 128), 128)]

    def up(n):
        k, h = n // 2, n % 2
        source = jnp.maximum(2 * k - 1, 0)
        return remote(half(lines, source, h), half(lines, 2 * k + 1, h), up_sent.at[n], up_got.at[n], relative(0, 0, 7, 0))

    def down(n):
        k, h = n // 2, 1 - n % 2
        return remote(
            half(lines, 2 * k, h), half(lines, jnp.minimum(2 * k + 2, 7), h),
            down_sent.at[n], down_got.at[n], relative(0, 0, 1, 0),
        )

    def up_label(k):
        source = jnp.maximum(2 * k - 1, 0)
        i = 2 * k + 1
        return remote(line_labels.at[source], line_labels.at[i], line_label_sent.at[i], line_label_got.at[i], relative(0, 0, 7, 0))

    def down_label(k):
        i = 2 * k + 2
        return remote(line_labels.at[2 * k], line_labels.at[i], line_label_sent.at[i], line_label_got.at[i], relative(0, 0, 1, 0))

    def between(k):
        (x, y), (a, b) = PLANE[k], PLANE[SOURCE[k]]
        return relative((a - x) % 4, (b - y) % 4, 0, 0)

    def plane(k, h):
        return remote(
            half(columns, 2 * SOURCE[k], h), half(columns, 2 * k, h),
            plane_sent.at[k, h], plane_got.at[k, h], between(k),
        )

    def plane_label(k):
        return remote(
            column_labels.at[2 * SOURCE[k]], column_labels.at[2 * k],
            plane_label_sent.at[k], plane_label_got.at[k], between(k),
        )

    def across(k):
        return remote(
            columns.at[2 * k], columns.at[2 * k + 1], across_sent.at[k], across_got.at[k], relative(0, 0, 0, 1)
        )

    def across_label(k):
        return remote(
            column_labels.at[2 * k], column_labels.at[2 * k + 1],
            across_label_sent.at[k], across_label_got.at[k], relative(0, 0, 0, 1),
        )

    near = [k for k in range(1, len(PLANE)) if LANDS[k] == 0]
    for h in (0, 1):
        up(jnp.int32(h)).start()
        down(jnp.int32(h)).start()
        for k in near:
            plane(k, h).start()
        if h == 0:
            up_label(jnp.int32(0)).start()
            down_label(jnp.int32(0)).start()
            for k in near:
                plane_label(k).start()
    across(0).start()
    across_label(0).start()

    line_best[...] = jnp.full(line_best.shape, -1.0, jnp.float32)
    column_best[...] = jnp.full(column_best.shape, -1.0, jnp.float32)
    odd[...] = jnp.full(odd.shape, -1.0, jnp.float32)

    def spread(r):
        for top in (0, 128):
            column = jnp.broadcast_to(line_labels[r, :, top : top + 128], (128, 128)).T
            line_place[r, top : top + 128, :] = column
            line_order[r, top : top + 128, :] = (column & (SPAN - 1)) + LOWEST

    spread(0)
    even[...] = scores(lines, 0, columns, 0)
    keep_best(even, 0, 0, column_labels, line_place, line_order, line_best, column_best, same_rows=True)

    counts = [count for step in GROUPS for count in step]
    starts = [sum(counts[:m]) for m in range(len(counts) + 1)]
    coded = [r * 128 + c * 4 + bit for r, c, bit in TILES]
    words = [
        [sum(t << (10 * j) for j, t in enumerate(coded[i + first : min(i + first + 3, i + GROUP)])) for i in range(0, len(coded), GROUP)]
        for first in range(0, GROUP, 3)
    ]
    x, y, z, _ = whereabouts()
    bits = z // 4 * 2 + x // 2 * 4 + y // 2 * 8

    def line_answer(r):
        return remote(
            line_answers.at[r], line_got.at[r], line_answer_sent.at[r], line_answer_got.at[r],
            relative(0, 0, LINES[r], 0),
        )

    def answer_line(r):
        line_answers[r] = jnp.max(line_best[r].T, axis=0, keepdims=True)
        if r:
            line_answer(r).start()

    def arrivals(n):
        k, h = n // 2, n % 2
        up(n).wait_recv()
        down(n).wait_recv()

        @pl.when(n < STEPS - 2)
        def _():
            up(n + 2).start()
            down(n + 2).start()

        for at in (0, 2, 4):
            landing = [j for j in range(1, len(PLANE)) if LANDS[j] == at]
            onward = [j for j in range(1, len(PLANE)) if LANDS[j] == at + 2]

            @pl.when((n == at) | (n == at + 1))
            def _():
                for j in landing:
                    plane(j, h).wait_recv()
                for j in onward:
                    plane(j, h).start()

            @pl.when(n == at)
            def _():
                for j in landing:
                    plane_label(j).wait_recv()
                for j in onward:
                    plane_label(j).start()

            @pl.when(n == at + 1)
            def _():
                for j in landing:
                    across(j).start()
                    across_label(j).start()

        @pl.when(h == 0)
        def _():
            up_label(k).wait_recv()

            @pl.when(k < 3)
            def _():
                up_label(k + 1).start()
                down_label(k).wait_recv()

            @pl.when(k < 2)
            def _():
                down_label(k + 1).start()

        @pl.when(n == 6)
        def _():
            spread(7)

        @pl.when(h == 1)
        def _():
            spread(2 * k + 1)
            spread(2 * k + 2)

    def from_sibling(n):
        for at in (0, 1, 3, 5):

            @pl.when(n == at)
            def _():
                for j in range(len(PLANE)):
                    if (LANDS[j] + 1 if j else 0) == at:
                        across(j).wait_recv()
                        across_label(j).wait_recv()

    def step(m, before):
        n = m // 2

        @pl.when(m % 2 == 0)
        def _():
            arrivals(n)

        @pl.when(m % 2 == 1)
        def _():
            from_sibling(n)

        def group(u, carry):
            last_r, last_c = carry
            held = [pick(word, u) for word in words]
            for i in range(GROUP):
                code = (held[i // 3] >> (10 * (i % 3))) & 1023
                r = code >> 7
                c = ((code >> 2) & 31) + ((bits >> (code & 3)) & 1)
                now, then = (even, odd) if i % 2 == 0 else (odd, even)
                now[...] = scores(lines, r, columns, c)
                keep_best(then, last_r, last_c, column_labels, line_place, line_order, line_best, column_best)
                last_r, last_c = r, c
            return last_r, last_c

        return lax.fori_loop(pick(starts, m), pick(starts[1:], m), group, before)

    last_r, last_c = lax.fori_loop(0, len(counts), step, (jnp.int32(0), jnp.int32(0)))
    keep_best(odd, last_r, last_c, column_labels, line_place, line_order, line_best, column_best)

    def column_best_of(c):
        return jnp.max(column_best[c], axis=0, keepdims=True)

    for g in range(len(PLANE)):
        other_answers[g] = column_best_of(2 * g + 1)
    to_sibling = remote(other_answers, sibling_in, sibling_sent, sibling_got, relative(0, 0, 0, 1))
    to_sibling.start()

    def plane_answer(g):
        return remote(
            same_answers.at[g], column_got.at[g], plane_answer_sent.at[g], plane_answer_got.at[g],
            relative(*PLANE[g], 0, 0),
        )

    for r in range(8):
        answer_line(r)
    to_sibling.wait_recv()
    for g in range(len(PLANE)):
        same_answers[g] = jnp.maximum(column_best_of(2 * g), sibling_in[g])
        if g:
            plane_answer(g).start()
    best = jnp.maximum(line_answers[0], same_answers[0])
    for r in range(1, 8):
        line_answer(r).wait_recv()
        best = jnp.maximum(best, line_got[r])
    for g in range(1, len(PLANE)):
        plane_answer(g).wait_recv()
        best = jnp.maximum(best, column_got[g])
    out_ref[...] = best

    to_sibling.wait_send()
    for r in range(1, 8):
        line_answer(r).wait_send()
    for g in range(1, len(PLANE)):
        plane_answer(g).wait_send()
        plane_label(g).wait_send()
        for h in (0, 1):
            plane(g, h).wait_send()
    for g in range(len(PLANE)):
        across(g).wait_send()
        across_label(g).wait_send()
    for n in range(STEPS):
        up(jnp.int32(n)).wait_send()
        down(jnp.int32(n)).wait_send()
    for k in range(4):
        up_label(jnp.int32(k)).wait_send()
    for k in range(3):
        down_label(jnp.int32(k)).wait_send()


def on_device(embeddings, assignment, ordering):
    rows, features = embeddings.shape
    plane = len(PLANE)
    dma = pltpu.SemaphoreType.DMA
    best = pl.pallas_call(
        kernel,
        out_shape=jax.ShapeDtypeStruct((1, rows), jnp.float32),
        in_specs=[pl.BlockSpec(memory_space=pltpu.HBM)] * 3,
        out_specs=pl.BlockSpec(memory_space=pltpu.VMEM),
        scratch_shapes=[
            pltpu.VMEM((rows, features), jnp.bfloat16),
            pltpu.VMEM((1, rows), jnp.int32),
            pltpu.VMEM((1, rows), jnp.int32),
            dma((3,)),
            pltpu.VMEM((8, rows, features), jnp.bfloat16),
            pltpu.VMEM((2 * plane, rows, features), jnp.bfloat16),
            pltpu.VMEM((8, 1, rows), jnp.int32),
            pltpu.VMEM((2 * plane, 1, rows), jnp.int32),
            pltpu.VMEM((8, rows, 128), jnp.int32),
            pltpu.VMEM((8, rows, 128), jnp.int32),
            pltpu.VMEM((8, rows, 128), jnp.float32),
            pltpu.VMEM((2 * plane, 8, rows), jnp.float32),
            pltpu.VMEM((rows, rows), jnp.float32),
            pltpu.VMEM((rows, rows), jnp.float32),
            pltpu.VMEM((8, 1, rows), jnp.float32),
            pltpu.VMEM((plane, 1, rows), jnp.float32),
            pltpu.VMEM((plane, 1, rows), jnp.float32),
            pltpu.VMEM((plane, 1, rows), jnp.float32),
            pltpu.VMEM((8, 1, rows), jnp.float32),
            pltpu.VMEM((plane, 1, rows), jnp.float32),
            *[dma((STEPS,))] * 4,
            *[dma((8,))] * 2,
            *[dma((plane, 2))] * 2,
            *[dma((plane,))] * 2,
            *[dma((plane,))] * 4,
            *[dma((8,))] * 2,
            *[dma((plane,))] * 2,
            *[dma(())] * 2,
        ],
        compiler_params=pltpu.CompilerParams(
            collective_id=0, has_side_effects=True, vmem_limit_bytes=48 * 2**20
        ),
        cost_estimate=pl.CostEstimate(
            flops=2 * 136 * rows * rows * features, bytes_accessed=rows * features * 2, transcendentals=rows
        ),
    )(embeddings, assignment.reshape(1, rows), ordering.reshape(1, rows))
    return best.reshape(rows)


def solution(mesh):
    in_specs = (P(("clus", "rep"), None), P(("clus", "rep"), None), P(("clus", "rep")))
    out_specs = P(("clus", "rep"))
    return jax.shard_map(
        on_device, mesh=mesh, in_specs=in_specs, out_specs=out_specs, check_vma=False
    )
```

```python
import jax
import jax.numpy as jnp
from jax import lax
from jax.experimental import pallas as pl
from jax.experimental.pallas import tpu as pltpu
from jax.sharding import PartitionSpec as P

PLANE = ((0, 0), (1, 0), (0, 1), (3, 3), (2, 0), (0, 2), (3, 2), (2, 3), (2, 2), (1, 3))
LINES = (0, 1, 7, 2, 6, 3, 5, 4)
SOURCE = (None, 0, 0, 0, 1, 2, 3, 3, 6, 1)
LANDS = (None, 0, 0, 0, 2, 2, 2, 2, 4, 4)


def both(*units):
    return [(r, 2 * g + c, 0) for r, g in units for c in (0, 1)]


BY_Z, BY_X, BY_Y = 1, 2, 3
GROUP = 8
TILES = (
    [(0, 1, 0)] + both(*((0, g) for g in (1, 2, 3)), *((1, g) for g in range(4)), (2, 1), (2, 2), (2, 3))
    + both(*((3, g) for g in range(4)), *((4, g) for g in (1, 2, 3)))
    + [(0, 8, BY_X), (0, 10, BY_Y)] + both((2, 6), (2, 7), (0, 6), (0, 7), *((1, g) for g in (4, 5, 6, 7)))
    + both(*((3, g) for g in (4, 5, 6, 7)), (4, 6), (4, 7))
    + both(*((5, g) for g in range(8)), *((6, g) for g in (1, 2, 3, 6, 7)))
    + both(*((7, g) for g in (1, 2, 3, 6, 7))) + [(7, 2 * g, BY_Z) for g in (0, 4, 5)]
    + [(0, 16, BY_X), (7, 16, BY_Z)] + both(*((r, 8) for r in (1, 3, 5)), *((r, 9) for r in range(8)))
)
GROUPS = ((0, 0), (0, 2), (0, 0), (2, 2), (2, 0), (3, 0), (2, 3))
STEPS = len(GROUPS)
MESH = pl.DeviceIdType.MESH
LOWEST, HIGHEST = -(2**31), 2**31 - 1
SPAN = 65536


def whereabouts():
    clus, rep = lax.axis_index("clus"), lax.axis_index("rep")
    return (clus // 2) % 4, (clus // 8) * 2 + rep // 8, rep % 8, clus % 2


def relative(dx, dy, dz, other):
    x, y, z, core = whereabouts()
    x, y, z, core = (x + dx) % 4, (y + dy) % 4, (z + dz) % 8, (core + other) % 2
    return ((y // 2) * 4 + x) * 2 + core, (y % 2) * 8 + z


def pick(table, n):
    value = jnp.int32(table[0])
    for i in range(1, len(table)):
        value = jnp.where(n == i, jnp.int32(table[i]), value)
    return value


def scores(lines, r, columns, c):
    return lax.dot_general(
        lines[r], columns[c], (((1,), (1,)), ((), ())), preferred_element_type=jnp.float32
    )


def keep_best(s, r, c, column_labels, line_place, line_order, line_best, column_best, same_rows=False):
    label = column_labels[c]
    wide = []
    for left in (0, 128):
        p = label[:, left : left + 128]
        wide.append(
            [
                jnp.broadcast_to(p + LOWEST, (8, 128)),
                jnp.broadcast_to(HIGHEST - (p & (SPAN - 1)), (8, 128)),
                jnp.full((8, 128), -1.0, jnp.float32),
            ]
        )
    for top in range(0, 256, 8):
        mine, order = line_place[r, top : top + 8, :], line_order[r, top : top + 8, :]
        best = line_best[r, top : top + 8, :]
        for i, left in enumerate((0, 128)):
            theirs, limit, down = wide[i]
            ahead = mine - theirs
            v = s[top : top + 8, left : left + 128]
            earlier = ahead <= order
            if same_rows:
                earlier &= ahead != LOWEST
            best = jnp.maximum(best, jnp.where(earlier, v, -1.0))
            wide[i][2] = jnp.maximum(down, jnp.where(ahead > limit, v, -1.0))
        line_best[r, top : top + 8, :] = best
    for i, left in enumerate((0, 128)):
        here = column_best.at[c, :, pl.ds(left, 128)]
        here[...] = jnp.maximum(here[...], wide[i][2])


def kernel(
    rows_hbm, cluster_hbm, order_hbm, out_ref, rows_ref, cluster_ref, order_ref, loaded,
    lines, columns, line_labels, column_labels, line_place, line_order, line_best, column_best, even, odd,
    line_answers, same_answers, other_answers, sibling_in, line_got, column_got,
    up_sent, up_got, down_sent, down_got, line_label_sent, line_label_got,
    plane_sent, plane_got, plane_label_sent, plane_label_got,
    across_sent, across_got, across_label_sent, across_label_got,
    line_answer_sent, line_answer_got, plane_answer_sent, plane_answer_got, sibling_sent, sibling_got,
):
    def remote(src, dst, sent, got, device):
        return pltpu.make_async_remote_copy(src, dst, sent, got, device_id=device, device_id_type=MESH)

    loads = [
        pltpu.make_async_copy(src, dst, loaded.at[i])
        for i, (src, dst) in enumerate(((rows_hbm, rows_ref), (cluster_hbm, cluster_ref), (order_hbm, order_ref)))
    ]
    for load in loads:
        load.start()
    barrier = pltpu.get_barrier_semaphore()
    hello = {(0, 0, 1, 0), (0, 0, 7, 0), (0, 0, 0, 1)}
    for k in range(1, len(PLANE)):
        (x, y), (a, b) = PLANE[k], PLANE[SOURCE[k]]
        hello.add(((x - a) % 4, (y - b) % 4, 0, 0))
    for offset in sorted(hello):
        pl.semaphore_signal(barrier, inc=1, device_id=relative(*offset), device_id_type=MESH)

    loads[0].wait()
    for top in range(0, 256, 32):
        wide = rows_ref[top : top + 32, :].astype(jnp.float32)
        scale = lax.rsqrt(jnp.sum(wide * wide, axis=1, keepdims=True) + 1e-06)
        unit = (wide * scale).astype(jnp.bfloat16)
        lines[0, top : top + 32, :] = unit
        columns[0, top : top + 32, :] = unit
    loads[1].wait()
    loads[2].wait()
    place = cluster_ref[...] * SPAN + order_ref[...]
    line_labels[0] = place
    column_labels[0] = place
    pl.semaphore_wait(barrier, len(hello))

    def half(ref, slot, h):
        return ref.at[slot, pl.ds(pl.multiple_of(h * 128, 128), 128)]

    def up(n):
        k, h = n // 2, n % 2
        source = jnp.maximum(2 * k - 1, 0)
        return remote(half(lines, source, h), half(lines, 2 * k + 1, h), up_sent.at[n], up_got.at[n], relative(0, 0, 7, 0))

    def down(n):
        k, h = n // 2, 1 - n % 2
        return remote(
            half(lines, 2 * k, h), half(lines, jnp.minimum(2 * k + 2, 7), h),
            down_sent.at[n], down_got.at[n], relative(0, 0, 1, 0),
        )

    def up_label(k):
        source = jnp.maximum(2 * k - 1, 0)
        i = 2 * k + 1
        return remote(line_labels.at[source], line_labels.at[i], line_label_sent.at[i], line_label_got.at[i], relative(0, 0, 7, 0))

    def down_label(k):
        i = 2 * k + 2
        return remote(line_labels.at[2 * k], line_labels.at[i], line_label_sent.at[i], line_label_got.at[i], relative(0, 0, 1, 0))

    def between(k):
        (x, y), (a, b) = PLANE[k], PLANE[SOURCE[k]]
        return relative((a - x) % 4, (b - y) % 4, 0, 0)

    def plane(k, h):
        return remote(
            half(columns, 2 * SOURCE[k], h), half(columns, 2 * k, h),
            plane_sent.at[k, h], plane_got.at[k, h], between(k),
        )

    def plane_label(k):
        return remote(
            column_labels.at[2 * SOURCE[k]], column_labels.at[2 * k],
            plane_label_sent.at[k], plane_label_got.at[k], between(k),
        )

    def across(k):
        return remote(
            columns.at[2 * k], columns.at[2 * k + 1], across_sent.at[k], across_got.at[k], relative(0, 0, 0, 1)
        )

    def across_label(k):
        return remote(
            column_labels.at[2 * k], column_labels.at[2 * k + 1],
            across_label_sent.at[k], across_label_got.at[k], relative(0, 0, 0, 1),
        )

    near = [k for k in range(1, len(PLANE)) if LANDS[k] == 0]
    for h in (0, 1):
        up(jnp.int32(h)).start()
        down(jnp.int32(h)).start()
        for k in near:
            plane(k, h).start()
        if h == 0:
            up_label(jnp.int32(0)).start()
            down_label(jnp.int32(0)).start()
            for k in near:
                plane_label(k).start()
    across(0).start()
    across_label(0).start()

    line_best[...] = jnp.full(line_best.shape, -1.0, jnp.float32)
    column_best[...] = jnp.full(column_best.shape, -1.0, jnp.float32)
    odd[...] = jnp.full(odd.shape, -1.0, jnp.float32)

    def spread(r):
        for top in (0, 128):
            column = jnp.broadcast_to(line_labels[r, :, top : top + 128], (128, 128)).T
            line_place[r, top : top + 128, :] = column
            line_order[r, top : top + 128, :] = (column & (SPAN - 1)) + LOWEST

    spread(0)
    even[...] = scores(lines, 0, columns, 0)
    keep_best(even, 0, 0, column_labels, line_place, line_order, line_best, column_best, same_rows=True)

    counts = [count for step in GROUPS for count in step]
    starts = [sum(counts[:m]) for m in range(len(counts) + 1)]
    coded = [r * 128 + c * 4 + bit for r, c, bit in TILES]
    words = [
        [sum(t << (10 * j) for j, t in enumerate(coded[i + first : min(i + first + 3, i + GROUP)])) for i in range(0, len(coded), GROUP)]
        for first in range(0, GROUP, 3)
    ]
    x, y, z, _ = whereabouts()
    bits = z // 4 * 2 + x // 2 * 4 + y // 2 * 8

    def line_answer(r):
        return remote(
            line_answers.at[r], line_got.at[r], line_answer_sent.at[r], line_answer_got.at[r],
            relative(0, 0, LINES[r], 0),
        )

    def answer_line(r):
        line_answers[r] = jnp.max(line_best[r].T, axis=0, keepdims=True)
        if r:
            line_answer(r).start()

    def arrivals(n):
        k, h = n // 2, n % 2
        up(n).wait_recv()
        down(n).wait_recv()

        @pl.when(n < STEPS - 2)
        def _():
            up(n + 2).start()
            down(n + 2).start()

        for at in (0, 2, 4):
            landing = [j for j in range(1, len(PLANE)) if LANDS[j] == at]
            onward = [j for j in range(1, len(PLANE)) if LANDS[j] == at + 2]

            @pl.when((n == at) | ((n == at + 1) & (at < 4)))
            def _():
                for j in landing:
                    plane(j, h).wait_recv()
                for j in onward:
                    plane(j, h).start()

            @pl.when(n == at)
            def _():
                for j in landing:
                    plane_label(j).wait_recv()
                for j in onward:
                    plane_label(j).start()

            @pl.when((n == at + 1) & (at < 4))
            def _():
                for j in landing:
                    across(j).start()
                    across_label(j).start()

        @pl.when(h == 0)
        def _():
            up_label(k).wait_recv()

            @pl.when(k < 3)
            def _():
                up_label(k + 1).start()
                down_label(k).wait_recv()

            @pl.when(k < 2)
            def _():
                down_label(k + 1).start()

        @pl.when(n == 6)
        def _():
            spread(7)

        @pl.when(h == 1)
        def _():
            spread(2 * k + 1)
            spread(2 * k + 2)

    def from_sibling(n):
        last = [j for j in range(1, len(PLANE)) if LANDS[j] == 4]

        @pl.when(n == 5)
        def _():
            for j in last:
                plane(j, 1).wait_recv()
                across(j).start()
                across_label(j).start()

        for at in (0, 1, 3, 6):

            @pl.when(n == at)
            def _():
                for j in range(len(PLANE)):
                    if (0 if j == 0 else 6 if j in last else LANDS[j] + 1) == at:
                        across(j).wait_recv()
                        across_label(j).wait_recv()

    def step(m, before):
        n = m // 2

        @pl.when(m % 2 == 0)
        def _():
            arrivals(n)

        @pl.when(m % 2 == 1)
        def _():
            from_sibling(n)

        def group(u, carry):
            last_r, last_c = carry
            held = [pick(word, u) for word in words]
            for i in range(GROUP):
                code = (held[i // 3] >> (10 * (i % 3))) & 1023
                r = code >> 7
                c = ((code >> 2) & 31) + ((bits >> (code & 3)) & 1)
                now, then = (even, odd) if i % 2 == 0 else (odd, even)
                now[...] = scores(lines, r, columns, c)
                keep_best(then, last_r, last_c, column_labels, line_place, line_order, line_best, column_best)
                last_r, last_c = r, c
            return last_r, last_c

        return lax.fori_loop(pick(starts, m), pick(starts[1:], m), group, before)

    last_r, last_c = lax.fori_loop(0, len(counts), step, (jnp.int32(0), jnp.int32(0)))
    keep_best(odd, last_r, last_c, column_labels, line_place, line_order, line_best, column_best)

    def column_best_of(c):
        return jnp.max(column_best[c], axis=0, keepdims=True)

    for g in range(len(PLANE)):
        other_answers[g] = column_best_of(2 * g + 1)
    to_sibling = remote(other_answers, sibling_in, sibling_sent, sibling_got, relative(0, 0, 0, 1))
    to_sibling.start()

    def plane_answer(g):
        return remote(
            same_answers.at[g], column_got.at[g], plane_answer_sent.at[g], plane_answer_got.at[g],
            relative(*PLANE[g], 0, 0),
        )

    for r in range(8):
        answer_line(r)
    to_sibling.wait_recv()
    for g in range(len(PLANE)):
        same_answers[g] = jnp.maximum(column_best_of(2 * g), sibling_in[g])
        if g:
            plane_answer(g).start()
    best = jnp.maximum(line_answers[0], same_answers[0])
    for r in range(1, 8):
        line_answer(r).wait_recv()
        best = jnp.maximum(best, line_got[r])
    for g in range(1, len(PLANE)):
        plane_answer(g).wait_recv()
        best = jnp.maximum(best, column_got[g])
    out_ref[...] = best

    to_sibling.wait_send()
    for r in range(1, 8):
        line_answer(r).wait_send()
    for g in range(1, len(PLANE)):
        plane_answer(g).wait_send()
        plane_label(g).wait_send()
        for h in (0, 1):
            plane(g, h).wait_send()
    for g in range(len(PLANE)):
        across(g).wait_send()
        across_label(g).wait_send()
    for n in range(STEPS):
        up(jnp.int32(n)).wait_send()
        down(jnp.int32(n)).wait_send()
    for k in range(4):
        up_label(jnp.int32(k)).wait_send()
    for k in range(3):
        down_label(jnp.int32(k)).wait_send()


def on_device(embeddings, assignment, ordering):
    rows, features = embeddings.shape
    plane = len(PLANE)
    dma = pltpu.SemaphoreType.DMA
    best = pl.pallas_call(
        kernel,
        out_shape=jax.ShapeDtypeStruct((1, rows), jnp.float32),
        in_specs=[pl.BlockSpec(memory_space=pltpu.HBM)] * 3,
        out_specs=pl.BlockSpec(memory_space=pltpu.VMEM),
        scratch_shapes=[
            pltpu.VMEM((rows, features), jnp.bfloat16),
            pltpu.VMEM((1, rows), jnp.int32),
            pltpu.VMEM((1, rows), jnp.int32),
            dma((3,)),
            pltpu.VMEM((8, rows, features), jnp.bfloat16),
            pltpu.VMEM((2 * plane, rows, features), jnp.bfloat16),
            pltpu.VMEM((8, 1, rows), jnp.int32),
            pltpu.VMEM((2 * plane, 1, rows), jnp.int32),
            pltpu.VMEM((8, rows, 128), jnp.int32),
            pltpu.VMEM((8, rows, 128), jnp.int32),
            pltpu.VMEM((8, rows, 128), jnp.float32),
            pltpu.VMEM((2 * plane, 8, rows), jnp.float32),
            pltpu.VMEM((rows, rows), jnp.float32),
            pltpu.VMEM((rows, rows), jnp.float32),
            pltpu.VMEM((8, 1, rows), jnp.float32),
            pltpu.VMEM((plane, 1, rows), jnp.float32),
            pltpu.VMEM((plane, 1, rows), jnp.float32),
            pltpu.VMEM((plane, 1, rows), jnp.float32),
            pltpu.VMEM((8, 1, rows), jnp.float32),
            pltpu.VMEM((plane, 1, rows), jnp.float32),
            *[dma((STEPS,))] * 4,
            *[dma((8,))] * 2,
            *[dma((plane, 2))] * 2,
            *[dma((plane,))] * 2,
            *[dma((plane,))] * 4,
            *[dma((8,))] * 2,
            *[dma((plane,))] * 2,
            *[dma(())] * 2,
        ],
        compiler_params=pltpu.CompilerParams(
            collective_id=0, has_side_effects=True, vmem_limit_bytes=48 * 2**20
        ),
        cost_estimate=pl.CostEstimate(
            flops=2 * 136 * rows * rows * features, bytes_accessed=rows * features * 2, transcendentals=rows
        ),
    )(embeddings, assignment.reshape(1, rows), ordering.reshape(1, rows))
    return best.reshape(rows)


def solution(mesh):
    in_specs = (P(("clus", "rep"), None), P(("clus", "rep"), None), P(("clus", "rep")))
    out_specs = P(("clus", "rep"))
    return jax.shard_map(
        on_device, mesh=mesh, in_specs=in_specs, out_specs=out_specs, check_vma=False
    )
```

```python
import jax
import jax.numpy as jnp
from jax import lax
from jax.experimental import pallas as pl
from jax.experimental.pallas import tpu as pltpu
from jax.sharding import PartitionSpec as P

PLANE = ((0, 0), (1, 0), (0, 1), (3, 3), (2, 0), (0, 2), (3, 2), (2, 3), (2, 2), (1, 3))
LINES = (0, 1, 7, 2, 6, 3, 5, 4)
SOURCE = (None, 0, 0, 0, 1, 2, 3, 3, 6, 1)
LANDS = (None, 0, 0, 0, 2, 2, 2, 2, 4, 4)


def both(*units):
    return [(r, 2 * g + c, 0) for r, g in units for c in (0, 1)]


BY_Z, BY_X, BY_Y = 1, 2, 3
GROUP = 8
TILES = (
    [(0, 1, 0)] + both(*((0, g) for g in (1, 2, 3)), *((1, g) for g in range(4)), (2, 1), (2, 2), (2, 3))
    + both(*((3, g) for g in range(4)), *((4, g) for g in (1, 2, 3)))
    + [(0, 8, BY_X), (0, 10, BY_Y)] + both((2, 6), (2, 7), (0, 6), (0, 7), *((1, g) for g in (4, 5, 6, 7)))
    + both(*((3, g) for g in (4, 5, 6, 7)), (4, 6), (4, 7))
    + both(*((5, g) for g in range(8)), *((6, g) for g in (1, 2, 3, 6, 7)))
    + both(*((7, g) for g in (1, 2, 3, 6, 7))) + [(7, 2 * g, BY_Z) for g in (0, 4, 5)]
    + [(0, 16, BY_X), (7, 16, BY_Z)] + both(*((r, 8) for r in (1, 3, 5)), *((r, 9) for r in range(8)))
)
GROUPS = ((0, 0), (0, 2), (0, 0), (2, 2), (2, 0), (3, 0), (2, 3))
STEPS = len(GROUPS)
MESH = pl.DeviceIdType.MESH
LOWEST, HIGHEST = -(2**31), 2**31 - 1
SPAN = 65536


def whereabouts():
    clus, rep = lax.axis_index("clus"), lax.axis_index("rep")
    return (clus // 2) % 4, (clus // 8) * 2 + rep // 8, rep % 8, clus % 2


def relative(dx, dy, dz, other):
    x, y, z, core = whereabouts()
    x, y, z, core = (x + dx) % 4, (y + dy) % 4, (z + dz) % 8, (core + other) % 2
    return ((y // 2) * 4 + x) * 2 + core, (y % 2) * 8 + z


def pick(table, n):
    value = jnp.int32(table[0])
    for i in range(1, len(table)):
        value = jnp.where(n == i, jnp.int32(table[i]), value)
    return value


def scores(lines, r, columns, c):
    return lax.dot_general(
        lines[r], columns[c], (((1,), (1,)), ((), ())), preferred_element_type=jnp.float32
    )


def keep_best(s, r, c, column_labels, line_place, line_order, line_best, column_best, same_rows=False):
    label = column_labels[c]
    wide = []
    for left in (0, 128):
        p = label[:, left : left + 128]
        wide.append(
            [
                jnp.broadcast_to(p + LOWEST, (8, 128)),
                jnp.broadcast_to(HIGHEST - (p & (SPAN - 1)), (8, 128)),
                jnp.full((8, 128), -1.0, jnp.float32),
            ]
        )
    for top in range(0, 256, 8):
        mine, order = line_place[r, top : top + 8, :], line_order[r, top : top + 8, :]
        best = line_best[r, top : top + 8, :]
        for i, left in enumerate((0, 128)):
            theirs, limit, down = wide[i]
            ahead = mine - theirs
            v = s[top : top + 8, left : left + 128]
            earlier = ahead <= order
            if same_rows:
                earlier &= ahead != LOWEST
            best = jnp.maximum(best, jnp.where(earlier, v, -1.0))
            wide[i][2] = jnp.maximum(down, jnp.where(ahead > limit, v, -1.0))
        line_best[r, top : top + 8, :] = best
    for i, left in enumerate((0, 128)):
        here = column_best.at[c, :, pl.ds(left, 128)]
        here[...] = jnp.maximum(here[...], wide[i][2])


def kernel(
    rows_ref, cluster_ref, order_ref, out_ref,
    lines, columns, line_labels, column_labels, line_place, line_order, line_best, column_best, even, odd,
    line_answers, same_answers, other_answers, sibling_in, line_got, column_got,
    up_sent, up_got, down_sent, down_got, line_label_sent, line_label_got,
    plane_sent, plane_got, plane_label_sent, plane_label_got,
    across_sent, across_got, across_label_sent, across_label_got,
    line_answer_sent, line_answer_got, plane_answer_sent, plane_answer_got, sibling_sent, sibling_got,
):
    def remote(src, dst, sent, got, device):
        return pltpu.make_async_remote_copy(src, dst, sent, got, device_id=device, device_id_type=MESH)

    barrier = pltpu.get_barrier_semaphore()
    hello = {(0, 0, 1, 0), (0, 0, 7, 0), (0, 0, 0, 1)}
    for k in range(1, len(PLANE)):
        (x, y), (a, b) = PLANE[k], PLANE[SOURCE[k]]
        hello.add(((x - a) % 4, (y - b) % 4, 0, 0))
    for offset in sorted(hello):
        pl.semaphore_signal(barrier, inc=1, device_id=relative(*offset), device_id_type=MESH)

    for top in range(0, 256, 32):
        wide = rows_ref[top : top + 32, :].astype(jnp.float32)
        scale = lax.rsqrt(jnp.sum(wide * wide, axis=1, keepdims=True) + 1e-06)
        unit = (wide * scale).astype(jnp.bfloat16)
        lines[0, top : top + 32, :] = unit
        columns[0, top : top + 32, :] = unit
    place = cluster_ref[...] * SPAN + order_ref[...]
    line_labels[0] = place
    column_labels[0] = place
    pl.semaphore_wait(barrier, len(hello))

    def half(ref, slot, h):
        return ref.at[slot, pl.ds(pl.multiple_of(h * 128, 128), 128)]

    def up(n):
        k, h = n // 2, n % 2
        source = jnp.maximum(2 * k - 1, 0)
        return remote(half(lines, source, h), half(lines, 2 * k + 1, h), up_sent.at[n], up_got.at[n], relative(0, 0, 7, 0))

    def down(n):
        k, h = n // 2, 1 - n % 2
        return remote(
            half(lines, 2 * k, h), half(lines, jnp.minimum(2 * k + 2, 7), h),
            down_sent.at[n], down_got.at[n], relative(0, 0, 1, 0),
        )

    def up_label(k):
        source = jnp.maximum(2 * k - 1, 0)
        i = 2 * k + 1
        return remote(line_labels.at[source], line_labels.at[i], line_label_sent.at[i], line_label_got.at[i], relative(0, 0, 7, 0))

    def down_label(k):
        i = 2 * k + 2
        return remote(line_labels.at[2 * k], line_labels.at[i], line_label_sent.at[i], line_label_got.at[i], relative(0, 0, 1, 0))

    def between(k):
        (x, y), (a, b) = PLANE[k], PLANE[SOURCE[k]]
        return relative((a - x) % 4, (b - y) % 4, 0, 0)

    def plane(k, h):
        return remote(
            half(columns, 2 * SOURCE[k], h), half(columns, 2 * k, h),
            plane_sent.at[k, h], plane_got.at[k, h], between(k),
        )

    def plane_label(k):
        return remote(
            column_labels.at[2 * SOURCE[k]], column_labels.at[2 * k],
            plane_label_sent.at[k], plane_label_got.at[k], between(k),
        )

    def across(k):
        return remote(
            columns.at[2 * k], columns.at[2 * k + 1], across_sent.at[k], across_got.at[k], relative(0, 0, 0, 1)
        )

    def across_label(k):
        return remote(
            column_labels.at[2 * k], column_labels.at[2 * k + 1],
            across_label_sent.at[k], across_label_got.at[k], relative(0, 0, 0, 1),
        )

    near = [k for k in range(1, len(PLANE)) if LANDS[k] == 0]
    for h in (0, 1):
        up(jnp.int32(h)).start()
        down(jnp.int32(h)).start()
        for k in near:
            plane(k, h).start()
        if h == 0:
            up_label(jnp.int32(0)).start()
            down_label(jnp.int32(0)).start()
            for k in near:
                plane_label(k).start()
    across(0).start()
    across_label(0).start()

    line_best[...] = jnp.full(line_best.shape, -1.0, jnp.float32)
    column_best[...] = jnp.full(column_best.shape, -1.0, jnp.float32)
    odd[...] = jnp.full(odd.shape, -1.0, jnp.float32)

    def spread(r):
        for top in (0, 128):
            column = jnp.broadcast_to(line_labels[r, :, top : top + 128], (128, 128)).T
            line_place[r, top : top + 128, :] = column
            line_order[r, top : top + 128, :] = (column & (SPAN - 1)) + LOWEST

    spread(0)
    even[...] = scores(lines, 0, columns, 0)
    keep_best(even, 0, 0, column_labels, line_place, line_order, line_best, column_best, same_rows=True)

    counts = [count for step in GROUPS for count in step]
    starts = [sum(counts[:m]) for m in range(len(counts) + 1)]
    coded = [r * 128 + c * 4 + bit for r, c, bit in TILES]
    words = [
        [sum(t << (10 * j) for j, t in enumerate(coded[i + first : min(i + first + 3, i + GROUP)])) for i in range(0, len(coded), GROUP)]
        for first in range(0, GROUP, 3)
    ]
    x, y, z, _ = whereabouts()
    bits = z // 4 * 2 + x // 2 * 4 + y // 2 * 8

    def line_answer(r):
        return remote(
            line_answers.at[r], line_got.at[r], line_answer_sent.at[r], line_answer_got.at[r],
            relative(0, 0, LINES[r], 0),
        )

    def answer_line(r):
        line_answers[r] = jnp.max(line_best[r].T, axis=0, keepdims=True)
        if r:
            line_answer(r).start()

    def arrivals(n):
        k, h = n // 2, n % 2
        up(n).wait_recv()
        down(n).wait_recv()

        @pl.when(n < STEPS - 2)
        def _():
            up(n + 2).start()
            down(n + 2).start()

        for at in (0, 2, 4):
            landing = [j for j in range(1, len(PLANE)) if LANDS[j] == at]
            onward = [j for j in range(1, len(PLANE)) if LANDS[j] == at + 2]

            @pl.when((n == at) | ((n == at + 1) & (at < 4)))
            def _():
                for j in landing:
                    plane(j, h).wait_recv()
                for j in onward:
                    plane(j, h).start()

            @pl.when(n == at)
            def _():
                for j in landing:
                    plane_label(j).wait_recv()
                for j in onward:
                    plane_label(j).start()

            @pl.when((n == at + 1) & (at < 4))
            def _():
                for j in landing:
                    across(j).start()
                    across_label(j).start()

        @pl.when(h == 0)
        def _():
            up_label(k).wait_recv()

            @pl.when(k < 3)
            def _():
                up_label(k + 1).start()
                down_label(k).wait_recv()

            @pl.when(k < 2)
            def _():
                down_label(k + 1).start()

        @pl.when(n == 6)
        def _():
            spread(7)

        @pl.when(h == 1)
        def _():
            spread(2 * k + 1)
            spread(2 * k + 2)

    def from_sibling(n):
        last = [j for j in range(1, len(PLANE)) if LANDS[j] == 4]

        @pl.when(n == 5)
        def _():
            for j in last:
                plane(j, 1).wait_recv()
                across(j).start()
                across_label(j).start()

        for at in (0, 1, 3, 6):

            @pl.when(n == at)
            def _():
                for j in range(len(PLANE)):
                    if (0 if j == 0 else 6 if j in last else LANDS[j] + 1) == at:
                        across(j).wait_recv()
                        across_label(j).wait_recv()

    def step(m, before):
        n = m // 2

        @pl.when(m % 2 == 0)
        def _():
            arrivals(n)

        @pl.when(m % 2 == 1)
        def _():
            from_sibling(n)

        def group(u, carry):
            last_r, last_c = carry
            held = [pick(word, u) for word in words]
            for i in range(GROUP):
                code = (held[i // 3] >> (10 * (i % 3))) & 1023
                r = code >> 7
                c = ((code >> 2) & 31) + ((bits >> (code & 3)) & 1)
                now, then = (even, odd) if i % 2 == 0 else (odd, even)
                now[...] = scores(lines, r, columns, c)
                keep_best(then, last_r, last_c, column_labels, line_place, line_order, line_best, column_best)
                last_r, last_c = r, c
            return last_r, last_c

        return lax.fori_loop(pick(starts, m), pick(starts[1:], m), group, before)

    last_r, last_c = lax.fori_loop(0, len(counts), step, (jnp.int32(0), jnp.int32(0)))
    keep_best(odd, last_r, last_c, column_labels, line_place, line_order, line_best, column_best)

    def column_best_of(c):
        return jnp.max(column_best[c], axis=0, keepdims=True)

    for g in range(len(PLANE)):
        other_answers[g] = column_best_of(2 * g + 1)
    to_sibling = remote(other_answers, sibling_in, sibling_sent, sibling_got, relative(0, 0, 0, 1))
    to_sibling.start()

    def plane_answer(g):
        return remote(
            same_answers.at[g], column_got.at[g], plane_answer_sent.at[g], plane_answer_got.at[g],
            relative(*PLANE[g], 0, 0),
        )

    for r in range(8):
        answer_line(r)
    to_sibling.wait_recv()
    for g in range(len(PLANE)):
        same_answers[g] = jnp.maximum(column_best_of(2 * g), sibling_in[g])
        if g:
            plane_answer(g).start()
    best = jnp.maximum(line_answers[0], same_answers[0])
    for r in range(1, 8):
        line_answer(r).wait_recv()
        best = jnp.maximum(best, line_got[r])
    for g in range(1, len(PLANE)):
        plane_answer(g).wait_recv()
        best = jnp.maximum(best, column_got[g])
    out_ref[...] = best

    to_sibling.wait_send()
    for r in range(1, 8):
        line_answer(r).wait_send()
    for g in range(1, len(PLANE)):
        plane_answer(g).wait_send()
        plane_label(g).wait_send()
        for h in (0, 1):
            plane(g, h).wait_send()
    for g in range(len(PLANE)):
        across(g).wait_send()
        across_label(g).wait_send()
    for n in range(STEPS):
        up(jnp.int32(n)).wait_send()
        down(jnp.int32(n)).wait_send()
    for k in range(4):
        up_label(jnp.int32(k)).wait_send()
    for k in range(3):
        down_label(jnp.int32(k)).wait_send()


def on_device(embeddings, assignment, ordering):
    rows, features = embeddings.shape
    plane = len(PLANE)
    dma = pltpu.SemaphoreType.DMA
    best = pl.pallas_call(
        kernel,
        out_shape=jax.ShapeDtypeStruct((1, rows), jnp.float32),
        in_specs=[pl.BlockSpec(memory_space=pltpu.VMEM)] * 3,
        out_specs=pl.BlockSpec(memory_space=pltpu.VMEM),
        scratch_shapes=[
            pltpu.VMEM((8, rows, features), jnp.bfloat16),
            pltpu.VMEM((2 * plane, rows, features), jnp.bfloat16),
            pltpu.VMEM((8, 1, rows), jnp.int32),
            pltpu.VMEM((2 * plane, 1, rows), jnp.int32),
            pltpu.VMEM((8, rows, 128), jnp.int32),
            pltpu.VMEM((8, rows, 128), jnp.int32),
            pltpu.VMEM((8, rows, 128), jnp.float32),
            pltpu.VMEM((2 * plane, 8, rows), jnp.float32),
            pltpu.VMEM((rows, rows), jnp.float32),
            pltpu.VMEM((rows, rows), jnp.float32),
            pltpu.VMEM((8, 1, rows), jnp.float32),
            pltpu.VMEM((plane, 1, rows), jnp.float32),
            pltpu.VMEM((plane, 1, rows), jnp.float32),
            pltpu.VMEM((plane, 1, rows), jnp.float32),
            pltpu.VMEM((8, 1, rows), jnp.float32),
            pltpu.VMEM((plane, 1, rows), jnp.float32),
            *[dma((STEPS,))] * 4,
            *[dma((8,))] * 2,
            *[dma((plane, 2))] * 2,
            *[dma((plane,))] * 2,
            *[dma((plane,))] * 4,
            *[dma((8,))] * 2,
            *[dma((plane,))] * 2,
            *[dma(())] * 2,
        ],
        compiler_params=pltpu.CompilerParams(
            collective_id=0, has_side_effects=True, vmem_limit_bytes=48 * 2**20
        ),
        cost_estimate=pl.CostEstimate(
            flops=2 * 136 * rows * rows * features, bytes_accessed=rows * features * 2, transcendentals=rows
        ),
    )(embeddings, assignment.reshape(1, rows), ordering.reshape(1, rows))
    return best.reshape(rows)


def solution(mesh):
    in_specs = (P(("clus", "rep"), None), P(("clus", "rep"), None), P(("clus", "rep")))
    out_specs = P(("clus", "rep"))
    return jax.shard_map(
        on_device, mesh=mesh, in_specs=in_specs, out_specs=out_specs, check_vma=False
    )
```
